32 devices in a mesh: gx: 4 (over y, x), gy: 8 (over z, core).
Axes of the slice: x: 2, y: 2, z: 4, core: 2. Of those that a mesh axis runs over, the one named last changes fastest.
Arguments:
- object_field: float32 [2, 2, 2048, 1024], P(None, None, 'gy', 'gx'), may hold values from -5 to 5
- probe: float32 [2, 256, 256], replicated, may hold values from -6 to 6
- positions: int32 [16, 4, 2], P('gy', 'gx'), may hold values from 0 to 256, as said below
- residual: bfloat16 [16, 4, 2, 256, 256], P('gy', 'gx'), may hold values from -6 to 6
- saved_wave: bfloat16 [16, 4, 2, 256, 256], P('gy', 'gx'), may hold values from -6 to 6
Outputs:
- new_object: float32 [2, 2, 2048, 1024], P(None, None, 'gy', 'gx')
The draws below stay inside these ranges and needn't reach their ends.
Inputs may be any that keep to these rules, and one draw needn't show every extreme that they name: `positions`: row and column of each position's window corner in a frame whose anchor lies 128 cells above and to the left of its tile's first cell, so that the window stays within 128 cells of the tile; position p of a tile lies near row 128 and column 128 * (1 + p mod 2) of that frame.
All inputs are finite; a program needn't handle non-finite values.
Results may differ from the reference program's by a relative error of at most 0.0003.
Values sent between devices are 32-bit elements; how exact they have to be, the bound alone decides.
No kernel may reach another device: no remote copies, remote signals or barrier semaphores. Data moves between devices by JAX's collectives and lax.ppermute only.
A program may use at most 64 MiB of HBM per device.

```python
import jax
import jax.numpy as jnp
from jax import lax

WIN = 256
PPD = 2
RIM = 128
TILE_ROWS = 8
TILE_COLS = 4
NR = 2048
NC = 1024


def draw_positions(key, part):
    total_rows = TILE_ROWS * PPD
    shape = (total_rows, TILE_COLS, 2)
    jitter = jax.random.randint(key, shape, -RIM, RIM + 1)
    within = jnp.arange(total_rows, dtype=jnp.int32) % PPD
    grid = jnp.stack([within // 2, within % 2], axis=-1)[:, None, :]
    anchor = jnp.clip(RIM + RIM * grid + jitter, 0, 2 * RIM)
    anchor = anchor.at[0, 0, 0].set(0)
    anchor = anchor.at[total_rows - 1, TILE_COLS - 1, 1].set(2 * RIM)
    return anchor.astype(jnp.int32)


def block_levels(own_key, extent, shards, low, top_value):
    level = 1.0
    for axis_at, blocks in shards:
        draws = jax.random.uniform(jax.random.fold_in(jax.random.fold_in(own_key, 6), axis_at), (blocks,), jnp.float32, low / len(shards), top_value / len(shards))
        level = level * jnp.repeat(jnp.exp(draws), extent[axis_at] // blocks).reshape((-1,) + (1,) * (len(extent) - 1 - axis_at))
    return level


def noise(rng, dims, deviation, reach, split=(), held_as=jnp.bfloat16):
    values = jax.random.normal(rng, dims, jnp.float32) * deviation
    if len(split) > 0:
        values = block_levels(rng, dims, split, -0.22, 0.18) * values
    return jnp.clip(values, min=-reach, max=reach).astype(held_as)


def setup_inputs(seed: int = 0) -> dict:
    key_of = jax.random.split(jax.random.key(seed), 6)
    return {
        "object_field": noise(key_of[0], (2, 2, NR, NC), 0.7, 5.0, ((2, 8), (3, 4)), jnp.float32),
        "probe": noise(key_of[1], (2, WIN, WIN), 1.0, 6.0, (), jnp.float32),
        "positions": draw_positions(jax.random.fold_in(key_of[5], 71), 0),
        "residual": noise(key_of[3], (PPD * TILE_ROWS, TILE_COLS, 2, WIN, WIN), 1.0, 6.0, ((0, 8), (1, 4))),
        "saved_wave": noise(key_of[4], (PPD * TILE_ROWS, TILE_COLS, 2, WIN, WIN), 1.0, 6.0, ((0, 8), (1, 4))),
    }


fresnel_rate = 200.0
ridge = 0.5


def kernel_conj(size):
    index = jnp.arange(size, dtype=jnp.int32)
    freq = (((index + size // 2) % size) - size // 2).astype(jnp.float32) / size
    phase = fresnel_rate * (freq[:, None] ** 2 + freq[None, :] ** 2)
    return jnp.cos(phase), jnp.sin(phase)


def reference(object_field, probe, positions, residual, saved_wave):
    rows_all = WIN * TILE_ROWS
    cols_all = WIN * TILE_COLS
    second = object_field[1, 0] + 1j * object_field[1, 1]
    padded = jnp.pad(second, RIM)
    probe_wave = probe[0] + 1j * probe[1]
    kernel_re, kernel_im = kernel_conj(WIN)
    back_kernel = kernel_re + 1j * kernel_im
    light = probe[0] * probe[0] + probe[1] * probe[1]
    initial = jnp.zeros((5, rows_all + 2 * RIM, cols_all + 2 * RIM), jnp.float32)

    def visit(carry, entry):
        row_block = entry // TILE_COLS
        column = entry % TILE_COLS
        tile_row = row_block // PPD
        top = (tile_row * WIN + positions[row_block, column, 0]).astype(jnp.int32)
        left = (column * WIN + positions[row_block, column, 1]).astype(jnp.int32)
        detector = residual[row_block, column].astype(jnp.float32)
        wave = saved_wave[row_block, column].astype(jnp.float32)
        field = jnp.fft.ifft2(detector[0] + 1j * detector[1], norm="ortho")
        patch = lax.dynamic_slice(padded, (top, left), (WIN, WIN))
        chi = jnp.conj(patch) * field
        back = jnp.fft.ifft2(back_kernel * jnp.fft.fft2(chi, norm="ortho"), norm="ortho")
        first_grad = jnp.conj(probe_wave) * back
        second_grad = jnp.conj(wave[0] + 1j * wave[1]) * field
        stacked = jnp.stack([first_grad.real, first_grad.imag, second_grad.real, second_grad.imag, light]).astype(carry.dtype)
        anchor = jnp.zeros((), jnp.int32)
        current = lax.dynamic_slice(carry, (anchor, top, left), (5, WIN, WIN))
        return lax.dynamic_update_slice(carry, current + stacked, (anchor, top, left)), None

    total_spots = TILE_ROWS * PPD * TILE_COLS
    carry, _ = lax.scan(visit, initial, jnp.arange(total_spots, dtype=jnp.int32))
    inner = carry[:, RIM:RIM + rows_all, RIM:RIM + cols_all]
    grads = inner[:4].reshape(2, 2, rows_all, cols_all)
    return object_field - grads / (inner[4] + ridge)
```

```python
import functools

import jax
import jax.numpy as jnp
import ml_dtypes
import numpy as np
from jax import lax
from jax.experimental import pallas as pl
from jax.experimental.pallas import tpu as pltpu
from jax.sharding import PartitionSpec as P

fresnel_rate = 200.0
ridge = 0.5
CHUNK = 32
F32 = jnp.float32
BF16 = jnp.bfloat16


def real_blocks(matrix):
    right = np.block([[matrix.real, matrix.imag], [-matrix.imag, matrix.real]])
    left = np.block([[matrix.real, -matrix.imag], [matrix.imag, matrix.real]])
    return right, left


def two_parts(table):
    high = table.astype(np.float32).astype(ml_dtypes.bfloat16)
    low = (table - high.astype(np.float64)).astype(ml_dtypes.bfloat16)
    return high, low


@functools.lru_cache(maxsize=None)
def tables(size):
    index = np.arange(size)
    inverse = np.exp(2j * np.pi * (np.outer(index, index) % size) / size) / np.sqrt(size)
    freq = ((index + size // 2) % size - size // 2) / size
    move = inverse @ np.diag(np.exp(1j * fresnel_rate * freq**2)) @ inverse.conj()
    out = []
    for matrix in (inverse, move):
        for table in real_blocks(matrix):
            out.extend(two_parts(table))
    return tuple(out)


def swap_pairs(count, first):
    pairs = []
    for low in range(first, count - 1, 2):
        pairs += [(low, low + 1), (low + 1, low)]
    return pairs


def swapped(value, axis, first):
    return lax.ppermute(value, axis, swap_pairs(lax.axis_size(axis), first))


def dot(a, b):
    return jnp.dot(a, b, preferred_element_type=F32)


def split(value):
    high = value.astype(BF16)
    return high, (value - high.astype(F32)).astype(BF16)


def place(waves, corners, out_first, out_second, out_middle, odd, window):
    half = window // 2

    def rows(base, lower, store):
        for start in range(0, half, CHUNK):
            at = pl.multiple_of(base + start, CHUNK)
            row = lax.broadcasted_iota(jnp.int32, (CHUNK, window), 0) + at
            col = lax.broadcasted_iota(jnp.int32, (CHUNK, window), 1)
            masks = []
            for r, c in corners:
                inside = (row < r) == (lower == 1)
                masks.append((inside & (col >= c), inside & (col < c)))
            for plane in range(len(waves)):
                left = right = None
                for number, (in_left, in_right) in enumerate(masks):
                    value = waves[plane][number, pl.ds(at, CHUNK), :]
                    a = jnp.where(in_left, value, 0.0)
                    b = jnp.where(in_right, value, 0.0)
                    left = a if left is None else left + a
                    right = b if right is None else right + b
                store(plane, start, left, right)

    def writer(ref, offset):
        def store(plane, start, left, right):
            ref[plane, offset + start : offset + start + CHUNK, :window] = left
            ref[plane, offset + start : offset + start + CHUNK, window:] = right

        return store

    rows((1 - odd) * half, 1 - odd, writer(out_first, 0))
    rows(odd * half, odd, writer(out_second, 0))
    rows(half, 0, writer(out_middle, 0))
    rows(0, 1, writer(out_middle, half))


def prepare(
    pos, residual, wave, probe, rt_hi, rt_lo, lt_hi, lt_lo,
    field, probes, first, second, middle,
    twice, inner_hi, inner_lo, outer, grads,
):
    window = probe.shape[-1]
    count = residual.shape[0]
    odd = lax.rem(lax.axis_index("gy"), 2)
    corners = [(pos[number, 0, 0], pos[number, 0, 1]) for number in range(count)]

    def rolled(value_at, corner, store):
        r, c = corner
        for start in range(0, window, CHUNK):
            value = pltpu.roll(value_at(start), c, 1)
            twice[start : start + CHUNK] = value
            twice[window + start : window + start + CHUNK] = value
        twice[2 * window :] = twice[:8]
        rest = lax.rem(window - r, 8)
        back = lax.rem(CHUNK + 8 - rest, CHUNK + 8)
        for start in range(0, window, CHUNK):
            value = twice[pl.ds(pl.multiple_of(window - r - rest + start, 8), CHUNK + 8), :]
            store(start, pltpu.roll(value, back, 0)[:CHUNK])

    for number in range(count):
        detector_re = residual[number, 0, 0]
        detector_im = residual[number, 0, 1]
        table_hi, table_lo = rt_hi[...], rt_lo[...]
        line = dot(detector_re, table_hi[:window]) + dot(detector_im, table_hi[window:])
        line += dot(detector_re, table_lo[:window]) + dot(detector_im, table_lo[window:])
        high, low = split(line)
        inner_hi[:window, number * window : (number + 1) * window] = high[:, :window]
        inner_hi[window:, number * window : (number + 1) * window] = high[:, window:]
        inner_lo[:window, number * window : (number + 1) * window] = low[:, :window]
        inner_lo[window:, number * window : (number + 1) * window] = low[:, window:]
    outer[...] = dot(lt_hi[...], inner_hi[...]) + dot(lt_lo[...], inner_hi[...]) + dot(lt_hi[...], inner_lo[...])

    for number, corner in enumerate(corners):
        for part in range(2):

            def from_outer(start):
                return outer[
                    part * window + start : part * window + start + CHUNK, number * window : (number + 1) * window
                ]

            def to_field(start, value):
                field[number, part, start : start + CHUNK] = value

            rolled(from_outer, corner, to_field)

            def from_probe(start):
                return probe[part, start : start + CHUNK]

            def to_probes(start, value):
                probes[number, part, start : start + CHUNK] = value

            rolled(from_probe, corner, to_probes)

        for part in range(2):

            def from_wave(start):
                return wave[number, 0, part, start : start + CHUNK].astype(F32)

            def to_grads(start, value):
                grads[part, number, start : start + CHUNK] = value

            rolled(from_wave, corner, to_grads)
        for start in range(0, window, CHUNK):
            rows = slice(start, start + CHUNK)
            wave_re, wave_im = grads[0, number, rows], grads[1, number, rows]
            field_re, field_im = field[number, 0, rows], field[number, 1, rows]
            grads[0, number, rows] = wave_re * field_re + wave_im * field_im
            grads[1, number, rows] = wave_re * field_im - wave_im * field_re
            probe_re, probe_im = probes[number, 0, rows], probes[number, 1, rows]
            grads[2, number, rows] = probe_re * probe_re + probe_im * probe_im
    place([grads.at[0], grads.at[1], grads.at[2]], corners, first, second, middle, odd, window)


def widen(second, from_first, from_second, first, second_out, middle):
    half = from_first.shape[-1]
    odd_x = lax.rem(lax.axis_index("gx"), 2)
    odd_y = lax.rem(lax.axis_index("gy"), 2)
    planes = second.shape[0]
    for plane in range(planes):
        middle[plane, :, half : 3 * half] = second[plane]
        middle[plane, :, pl.ds(pl.multiple_of((1 - odd_x) * 3 * half, half), half)] = from_first[plane]
        middle[plane, :, pl.ds(pl.multiple_of(odd_x * 3 * half, half), half)] = from_second[plane]
        first[plane] = middle[plane, pl.ds(pl.multiple_of((1 - odd_y) * half, half), half), :]
        second_out[plane] = middle[plane, pl.ds(pl.multiple_of(odd_y * half, half), half), :]


def propagate(
    pos, field, probes, middle_in, from_first, from_second, rm_hi, rm_lo, lm_hi, lm_lo,
    first, second, middle,
    chi_hi, chi_lo, inner_hi, inner_lo, outer, grads,
):
    window = field.shape[-1]
    half = window // 2
    count = field.shape[0]
    odd = lax.rem(lax.axis_index("gy"), 2)
    corners = [(pos[number, 0, 0], pos[number, 0, 1]) for number in range(count)]

    for start in range(0, window, CHUNK):
        rows = slice(start, start + CHUNK)
        row = lax.broadcasted_iota(jnp.int32, (CHUNK, window), 0) + start
        col = lax.broadcasted_iota(jnp.int32, (CHUNK, window), 1)
        upper, lower = [], []
        for part in range(2):
            if start < half:
                upper.append(jnp.where(odd == 1, from_first[part, rows], from_second[part, rows]))
                lower.append(middle_in[part, half + start : half + start + CHUNK])
            else:
                shifted = slice(start - half, start - half + CHUNK)
                upper.append(middle_in[part, shifted])
                lower.append(jnp.where(odd == 1, from_second[part, shifted], from_first[part, shifted]))
        for number, (r, c) in enumerate(corners):
            low_row, low_col = row < r, col < c
            patch = []
            for part in range(2):
                above = jnp.where(low_col, upper[part][:, window:], upper[part][:, :window])
                below = jnp.where(low_col, lower[part][:, window:], lower[part][:, :window])
                patch.append(jnp.where(low_row, below, above))
            field_re, field_im = field[number, 0, rows], field[number, 1, rows]
            at = slice(number * window + start, number * window + start + CHUNK)
            high, low = split(patch[0] * field_re + patch[1] * field_im)
            chi_hi[at, :window] = high
            chi_lo[at, :window] = low
            high, low = split(patch[0] * field_im - patch[1] * field_re)
            chi_hi[at, window:] = high
            chi_lo[at, window:] = low

    for number in range(count):
        rows = slice(number * window, (number + 1) * window)
        line = dot(chi_hi[rows], rm_hi[...]) + dot(chi_hi[rows], rm_lo[...]) + dot(chi_lo[rows], rm_hi[...])
        high, low = split(line)
        inner_hi[:window, rows] = high[:, :window]
        inner_hi[window:, rows] = high[:, window:]
        inner_lo[:window, rows] = low[:, :window]
        inner_lo[window:, rows] = low[:, window:]
    outer[...] = dot(lm_hi[...], inner_hi[...]) + dot(lm_lo[...], inner_hi[...]) + dot(lm_hi[...], inner_lo[...])

    for number in range(count):
        cols = slice(number * window, (number + 1) * window)
        for start in range(0, window, CHUNK):
            rows = slice(start, start + CHUNK)
            probe_re, probe_im = probes[number, 0, rows], probes[number, 1, rows]
            back_re = outer[start : start + CHUNK, cols]
            back_im = outer[window + start : window + start + CHUNK, cols]
            grads[0, number, rows] = probe_re * back_re + probe_im * back_im
            grads[1, number, rows] = probe_re * back_im - probe_im * back_re
    place([grads.at[0], grads.at[1]], corners, first, second, middle, odd, window)


def narrow(middle, from_first, from_second, first, second, centre):
    half = first.shape[-1]
    odd_x = lax.rem(lax.axis_index("gx"), 2)
    odd_y = lax.rem(lax.axis_index("gy"), 2)
    for plane in range(middle.shape[0]):
        for start in range(0, half, CHUNK):
            rows = slice(start, start + CHUNK)
            for received, base in ((from_first, (1 - odd_y) * half), (from_second, odd_y * half)):
                at = pl.ds(pl.multiple_of(base + start, CHUNK), CHUNK)
                total = middle[plane, at, :] + received[plane, rows]
                left, right = total[:, :half], total[:, 3 * half :]
                centre[plane, at, :] = total[:, half : 3 * half]
                first[plane, at, :] = jnp.where(odd_x == 1, left, right)
                second[plane, at, :] = jnp.where(odd_x == 1, right, left)


def joined(centre, from_first, from_second, plane, rows, odd_x):
    half = from_first.shape[-1]
    one, two = from_first[plane, rows], from_second[plane, rows]
    left = centre[plane, rows, :half] + jnp.where(odd_x == 1, one, two)
    right = centre[plane, rows, half:] + jnp.where(odd_x == 1, two, one)
    return left, right


def update(object_field, centre2, first2, second2, centre1, first1, second1, out):
    half = first2.shape[-1]
    window = centre2.shape[-1]
    odd_x = lax.rem(lax.axis_index("gx"), 2)
    for start in range(0, window, CHUNK):
        rows = slice(start, start + CHUNK)
        light = joined(centre2, first2, second2, 2, rows, odd_x)
        scale = [1.0 / (value + ridge) for value in light]
        for number, refs in enumerate(((centre1, first1, second1), (centre2, first2, second2))):
            for part in range(2):
                sides = joined(*refs, part, rows, odd_x)
                for side, cols in enumerate((slice(0, half), slice(half, None))):
                    out[number, part, rows, cols] = object_field[number, part, rows, cols] - sides[side] * scale[side]


VMEM = pl.BlockSpec(memory_space=pltpu.VMEM)
SMEM = pl.BlockSpec(memory_space=pltpu.SMEM)


def call(body, outs, in_specs, args, scratch=(), flops=0, name=None):
    moved = sum(x.size * x.dtype.itemsize for x in args) + sum(4 * int(np.prod(s)) for s in outs)
    return pl.pallas_call(
        body,
        out_shape=[jax.ShapeDtypeStruct(shape, F32) for shape in outs],
        in_specs=in_specs,
        out_specs=[VMEM] * len(outs),
        scratch_shapes=list(scratch),
        compiler_params=pltpu.CompilerParams(vmem_limit_bytes=40 * 1024 * 1024),
        cost_estimate=pl.CostEstimate(flops=flops, bytes_accessed=moved, transcendentals=0),
        name=name,
    )(*args)


def shards(object_field, probe, positions, residual, saved_wave):
    window = probe.shape[-1]
    half = window // 2
    count = positions.shape[0]
    odd_x = lax.rem(lax.axis_index("gx"), 2)
    rt_hi, rt_lo, lt_hi, lt_lo, rm_hi, rm_lo, lm_hi, lm_lo = (jnp.asarray(t) for t in tables(window))

    second = object_field[1]
    left, right = second[:, :, :half], second[:, :, half:]
    halo_first = swapped(jnp.where(odd_x == 1, left, right), "gx", 0)
    halo_second = swapped(jnp.where(odd_x == 1, right, left), "gx", 1)

    def pieces(planes):
        return [(planes, half, 2 * window), (planes, half, 2 * window), (planes, window, 2 * window)]

    def frame_scratch(planes):
        wide = (2 * window, count * window)
        return [
            pltpu.VMEM(wide, BF16),
            pltpu.VMEM(wide, BF16),
            pltpu.VMEM(wide, F32),
            pltpu.VMEM((planes, count, window, window), F32),
        ]

    fields, probes, up2, down2, middle2 = call(
        prepare,
        [(count, 2, window, window)] * 2 + pieces(3),
        [SMEM] + [VMEM] * 7,
        (positions, residual, saved_wave, probe, rt_hi, rt_lo, lt_hi, lt_lo),
        [pltpu.VMEM((2 * window + 8, window), F32)] + frame_scratch(3),
        flops=count * 5 * 2 * 4 * window**3,
        name="prepare",
    )
    from_up2 = swapped(up2, "gy", 0)
    from_down2 = swapped(down2, "gy", 1)

    up0, down0, wide0 = call(
        widen,
        pieces(2),
        [VMEM] * 3,
        (second, halo_first, halo_second),
        name="widen",
    )
    from_up0 = swapped(up0, "gy", 0)
    from_down0 = swapped(down0, "gy", 1)

    def strips(planes):
        return [(planes, window, half), (planes, window, half), (planes, window, window)]

    first2, second2, centre2 = call(
        narrow, strips(3), [VMEM] * 3, (middle2, from_up2, from_down2), name="narrow2"
    )
    got_first2 = swapped(first2, "gx", 0)
    got_second2 = swapped(second2, "gx", 1)

    up1, down1, middle1 = call(
        propagate,
        pieces(2),
        [SMEM] + [VMEM] * 9,
        (positions, fields, probes, wide0, from_up0, from_down0, rm_hi, rm_lo, lm_hi, lm_lo),
        [pltpu.VMEM((count * window, 2 * window), BF16)] * 2 + frame_scratch(2),
        flops=count * 6 * 2 * 4 * window**3,
        name="propagate",
    )
    from_up1 = swapped(up1, "gy", 0)
    from_down1 = swapped(down1, "gy", 1)
    first1, second1, centre1 = call(
        narrow, strips(2), [VMEM] * 3, (middle1, from_up1, from_down1), name="narrow1"
    )
    got_first1 = swapped(first1, "gx", 0)
    got_second1 = swapped(second1, "gx", 1)
    (new_object,) = call(
        update,
        [object_field.shape],
        [VMEM] * 7,
        (object_field, centre2, got_first2, got_second2, centre1, got_first1, got_second1),
        name="update",
    )
    return new_object


def solution(mesh):
    placed = (
        P(None, None, "gy", "gx"),
        P(),
        P("gy", "gx", None),
        P("gy", "gx", None, None, None),
        P("gy", "gx", None, None, None),
    )
    return jax.shard_map(
        shards, mesh=mesh, in_specs=placed, out_specs=P(None, None, "gy", "gx"), check_vma=False
    )
```

```python
import functools

import jax
import jax.numpy as jnp
import ml_dtypes
import numpy as np
from jax import lax
from jax.experimental import pallas as pl
from jax.experimental.pallas import tpu as pltpu
from jax.sharding import PartitionSpec as P

fresnel_rate = 200.0
ridge = 0.5
CHUNK = 32
F32 = jnp.float32
BF16 = jnp.bfloat16


def two_parts(table):
    high = table.astype(np.float32).astype(ml_dtypes.bfloat16)
    low = (table - high.astype(np.float64)).astype(ml_dtypes.bfloat16)
    return high, low


@functools.lru_cache(maxsize=None)
def tables(size):
    index = np.arange(size)
    inverse = np.exp(2j * np.pi * (np.outer(index, index) % size) / size) / np.sqrt(size)
    freq = ((index + size // 2) % size - size // 2) / size
    move = inverse @ np.diag(np.exp(1j * fresnel_rate * freq**2)) @ inverse.conj()
    out = []
    for matrix in (inverse, move):
        out.extend(two_parts(np.concatenate([matrix.real, matrix.imag], axis=1)))
    return tuple(out)


def swap_pairs(count, first):
    pairs = []
    for low in range(first, count - 1, 2):
        pairs += [(low, low + 1), (low + 1, low)]
    return pairs


def swapped(value, axis, first):
    return lax.ppermute(value, axis, swap_pairs(lax.axis_size(axis), first))


def dot(a, b):
    return jnp.dot(a, b, preferred_element_type=F32)


def split(value):
    high = value.astype(BF16)
    return high, (value - high.astype(F32)).astype(BF16)


def place(waves, corners, out_first, out_second, out_middle, odd, window):
    half = window // 2

    def rows(base, lower, store):
        for start in range(0, half, CHUNK):
            at = pl.multiple_of(base + start, CHUNK)
            row = lax.broadcasted_iota(jnp.int32, (CHUNK, window), 0) + at
            col = lax.broadcasted_iota(jnp.int32, (CHUNK, window), 1)
            masks = []
            for r, c in corners:
                inside = (row < r) == (lower == 1)
                masks.append((inside & (col >= c), inside & (col < c)))
            for plane in range(len(waves)):
                left = right = None
                for number, (in_left, in_right) in enumerate(masks):
                    value = waves[plane][number, pl.ds(at, CHUNK), :]
                    a = jnp.where(in_left, value, 0.0)
                    b = jnp.where(in_right, value, 0.0)
                    left = a if left is None else left + a
                    right = b if right is None else right + b
                store(plane, start, left, right)

    def writer(ref, offset):
        def store(plane, start, left, right):
            ref[plane, offset + start : offset + start + CHUNK, :window] = left
            ref[plane, offset + start : offset + start + CHUNK, window:] = right

        return store

    rows((1 - odd) * half, 1 - odd, writer(out_first, 0))
    rows(odd * half, odd, writer(out_second, 0))
    rows(half, 0, writer(out_middle, 0))
    rows(0, 1, writer(out_middle, half))


def from_right(rows_re, rows_im, high, low, passes):
    window = high.shape[0]
    sums = []
    for rows in (rows_re, rows_im):
        total = dot(rows[0], high[...]) + dot(rows[0], low[...])
        if passes == 3:
            total += dot(rows[1], high[...])
        sums.append(total)
    one, two = sums
    return one[:, :window] - two[:, window:], one[:, window:] + two[:, :window]


def from_left(high, low, inner_hi, inner_lo):
    window = high.shape[0]
    sums = []
    for part in range(2):
        cols = slice(part * window, (part + 1) * window)
        sums.append(dot(high[:, cols], inner_hi) + dot(low[:, cols], inner_hi) + dot(high[:, cols], inner_lo))
    one, two = sums
    return one[:, :window] - two[:, window:], one[:, window:] + two[:, :window]


def rolled(twice, corner, store, window):
    r, c = corner
    rest = lax.rem(window - r, 8)
    back = lax.rem(CHUNK + 8 - rest, CHUNK + 8)
    for start in range(0, window, CHUNK):
        value = twice[pl.ds(pl.multiple_of(window - r - rest + start, 8), CHUNK + 8), :]
        store(start, pltpu.roll(pltpu.roll(value, back, 0)[:CHUNK], c, 1))


def twofold(twice, start, value, window):
    rows = value.shape[0]
    twice[start : start + rows] = value
    twice[window + start : window + start + rows] = value
    if start == 0:
        twice[2 * window : 2 * window + 8] = value[:8]


def corners_of(pos, count):
    return [(pos[number, 0, 0], pos[number, 0, 1]) for number in range(count)]


def detect(pos, residual, wave, table_hi, table_lo, field, first, second, middle, twice, grads):
    window = residual.shape[-1]
    count = residual.shape[0]
    odd = lax.rem(lax.axis_index("gy"), 2)
    corners = corners_of(pos, count)
    for number, corner in enumerate(corners):
        line = from_right((residual[number, 0, 0],), (residual[number, 0, 1],), table_hi, table_lo, 2)
        high, low = split(jnp.concatenate(line, axis=1))
        field_re, field_im = from_left(table_hi, table_lo, high, low)
        field[number, 0] = field_re
        field[number, 1] = field_im
        for start in range(0, window, CHUNK):
            rows = slice(start, start + CHUNK)
            wave_re, wave_im = wave[number, 0, 0, rows].astype(F32), wave[number, 0, 1, rows].astype(F32)
            value_re, value_im = field[number, 0, rows], field[number, 1, rows]
            twofold(twice.at[number, 0], start, wave_re * value_re + wave_im * value_im, window)
            twofold(twice.at[number, 1], start, wave_re * value_im - wave_im * value_re, window)
        for part in range(2):

            def store(start, value):
                grads[part, number, start : start + CHUNK] = value

            rolled(twice.at[number, part], corner, store, window)
    place([grads.at[0], grads.at[1]], corners, first, second, middle, odd, window)
    for ref in (first, second):
        ref[0, window // 2 :] = notes_of(pos, count, 2 * window)


def roll_fields(pos, field, probe, field_out, probes, twice):
    window = probe.shape[-1]
    count = field.shape[0]
    for part in range(2):
        for start in range(0, window, CHUNK):
            twofold(twice.at[count, part], start, probe[part, start : start + CHUNK], window)
    for number, corner in enumerate(corners_of(pos, count)):
        for part in range(2):
            for start in range(0, window, CHUNK):
                twofold(twice.at[number, part], start, field[number, part, start : start + CHUNK], window)

            def to_field(start, value):
                field_out[number, part, start : start + CHUNK] = value

            rolled(twice.at[number, part], corner, to_field, window)

            def to_probes(start, value):
                probes[number, part, start : start + CHUNK] = value

            rolled(twice.at[count, part], corner, to_probes, window)


def notes_size(count):
    return -(-(1 + 2 * count) // 8) * 8


def notes_of(pos, count, width):
    size = notes_size(count)
    row = lax.broadcasted_iota(jnp.int32, (size, width), 0)
    notes = jnp.where(row == 0, 1, 0)
    for number in range(count):
        for part in range(2):
            notes = jnp.where(row == 1 + 2 * number + part, pos[number, 0, part], notes)
    return notes.astype(F32)


def widen(object_field, from_first, from_second, first, second_out, middle):
    half = from_first.shape[-1]
    odd_x = lax.rem(lax.axis_index("gx"), 2)
    odd_y = lax.rem(lax.axis_index("gy"), 2)
    at_first = pl.ds(pl.multiple_of((1 - odd_x) * 3 * half, half), half)
    at_second = pl.ds(pl.multiple_of(odd_x * 3 * half, half), half)
    for plane in range(middle.shape[0]):
        middle[plane, :, half : 3 * half] = object_field[1, plane]
        middle[plane, :, at_first] = from_first[plane]
        middle[plane, :, at_second] = from_second[plane]
        for ref, base in ((first, (1 - odd_y) * half), (second_out, odd_y * half)):
            ref[plane] = middle[plane, pl.ds(pl.multiple_of(base, half), half), :]


def propagate(
    pos, field, probes, middle_in, from_first, from_second, table_hi, table_lo,
    first, second, middle,
    chi_hi, chi_lo, grads,
):
    window = field.shape[-1]
    half = window // 2
    count = field.shape[0]
    odd = lax.rem(lax.axis_index("gy"), 2)
    corners = corners_of(pos, count)

    for start in range(0, window, CHUNK):
        rows = slice(start, start + CHUNK)
        row = lax.broadcasted_iota(jnp.int32, (CHUNK, window), 0) + start
        col = lax.broadcasted_iota(jnp.int32, (CHUNK, window), 1)
        upper, lower = [], []
        for part in range(2):
            if start < half:
                upper.append(jnp.where(odd == 1, from_first[part, rows], from_second[part, rows]))
                lower.append(middle_in[part, half + start : half + start + CHUNK])
            else:
                shifted = slice(start - half, start - half + CHUNK)
                upper.append(middle_in[part, shifted])
                lower.append(jnp.where(odd == 1, from_second[part, shifted], from_first[part, shifted]))
        for number, (r, c) in enumerate(corners):
            low_row, low_col = row < r, col < c
            patch = []
            for part in range(2):
                above = jnp.where(low_col, upper[part][:, window:], upper[part][:, :window])
                below = jnp.where(low_col, lower[part][:, window:], lower[part][:, :window])
                patch.append(jnp.where(low_row, below, above))
            field_re, field_im = field[number, 0, rows], field[number, 1, rows]
            high, low = split(patch[0] * field_re + patch[1] * field_im)
            chi_hi[number, 0, rows] = high
            chi_lo[number, 0, rows] = low
            high, low = split(patch[0] * field_im - patch[1] * field_re)
            chi_hi[number, 1, rows] = high
            chi_lo[number, 1, rows] = low

    for number in range(count):
        line = from_right(
            (chi_hi[number, 0], chi_lo[number, 0]), (chi_hi[number, 1], chi_lo[number, 1]), table_hi, table_lo, 3
        )
        high, low = split(jnp.concatenate(line, axis=1))
        back_re, back_im = from_left(table_hi, table_lo, high, low)
        probe_re, probe_im = probes[number, 0], probes[number, 1]
        grads[0, number] = probe_re * back_re + probe_im * back_im
        grads[1, number] = probe_re * back_im - probe_im * back_re
    place([grads.at[0], grads.at[1]], corners, first, second, middle, odd, window)


def illuminate(pos, probe, up, down, first, second, scale, twice, notes, sems):
    window = probe.shape[-1]
    half = window // 2
    count = pos.shape[0]
    size = notes_size(count)
    odd_x = lax.rem(lax.axis_index("gx"), 2)
    odd_y = lax.rem(lax.axis_index("gy"), 2)
    copies, at = [], 0
    for ref, start, rows in ((up, half, size), (down, half, size), (first, window, 3 * size), (second, window, 3 * size)):
        source = ref.at[0, pl.ds(start, rows), pl.ds(0, half)]
        copies.append(pltpu.make_async_copy(source, notes.at[pl.ds(at, rows), :], sems.at[len(copies)]))
        copies[-1].start()
        at += rows
    for start in range(0, window, CHUNK):
        rows = slice(start, start + CHUNK)
        twofold(twice, start, probe[0, rows] * probe[0, rows] + probe[1, rows] * probe[1, rows], window)
    for copy in copies:
        copy.wait()

    shifts = []
    for down in (-1, 0, 1):
        for along in (-1, 0, 1):
            if along == 0:
                base = (odd_y if down > 0 else 1 - odd_y) * size
            else:
                base = (2 + 3 * (odd_x if along > 0 else 1 - odd_x) + 1 + down) * size
            for number in range(count):
                if down == 0 and along == 0:
                    valid, r, c = 1, pos[number, 0, 0], pos[number, 0, 1]
                else:
                    valid, r, c = (
                        notes[base + row, 0].astype(jnp.int32) for row in (0, 1 + 2 * number, 2 + 2 * number)
                    )
                top = r - half + window * down
                left = c - half + window * along
                top = jnp.where(valid == 1, top, window)
                shifts.append((top, left, r, c))

    def rows_at(index, carry):
        start = index * CHUNK
        row = lax.broadcasted_iota(jnp.int32, (CHUNK, window), 0) + start
        col = lax.broadcasted_iota(jnp.int32, (CHUNK, window), 1)
        total = jnp.zeros((CHUNK, window), F32)
        for top, left, r, c in shifts:
            turn = lax.rem(2 * window - half - r, window)
            rest = lax.rem(turn, 8)
            value = twice[pl.ds(pl.multiple_of(turn - rest + start, 8), CHUNK + 8), :]
            value = pltpu.roll(value, lax.rem(CHUNK + 8 - rest, CHUNK + 8), 0)[:CHUNK]
            value = pltpu.roll(value, lax.rem(c + half, window), 1)
            inside = (row >= top) & (row < top + window) & (col >= left) & (col < left + window)
            total += jnp.where(inside, value, 0.0)
        scale[pl.ds(pl.multiple_of(start, CHUNK), CHUNK), :] = 1.0 / (total + ridge)
        return carry

    lax.fori_loop(0, window // CHUNK, rows_at, 0)


def narrow(pos, middle, from_first, from_second, first, second, centre):
    half = first.shape[-1]
    window = 2 * half
    odd_x = lax.rem(lax.axis_index("gx"), 2)
    odd_y = lax.rem(lax.axis_index("gy"), 2)
    for plane in range(middle.shape[0]):
        for start in range(0, half, CHUNK):
            rows = slice(start, start + CHUNK)
            for received, base in ((from_first, (1 - odd_y) * half), (from_second, odd_y * half)):
                at = pl.ds(pl.multiple_of(base + start, CHUNK), CHUNK)
                total = middle[plane, at, :] + received[plane, rows]
                left, right = total[:, :half], total[:, 3 * half :]
                centre[plane, at, :] = total[:, half : 3 * half]
                first[plane, at, :] = jnp.where(odd_x == 1, left, right)
                second[plane, at, :] = jnp.where(odd_x == 1, right, left)
    if first.shape[1] > window:
        size = from_first.shape[1] - half
        above = jnp.where(odd_y == 1, from_first[0, half:, :half], from_second[0, half:, :half])
        below = jnp.where(odd_y == 1, from_second[0, half:, :half], from_first[0, half:, :half])
        for ref in (first, second):
            ref[0, window : window + size] = above
            ref[0, window + size : window + 2 * size] = notes_of(pos, pos.shape[0], half)
            ref[0, window + 2 * size :] = below


def join(centre, from_first, from_second, out):
    window = centre.shape[-1]
    half = window // 2
    odd_x = lax.rem(lax.axis_index("gx"), 2)
    for plane in range(centre.shape[0]):
        for received, base in ((from_first, (1 - odd_x) * half), (from_second, odd_x * half)):
            at = pl.ds(pl.multiple_of(base, half), half)
            out[plane, :, at] = centre[plane, :, at] + received[plane, :window]


def update(object_field, scale, total2, centre1, first1, second1, out):
    window = centre1.shape[-1]
    half = window // 2
    odd_x = lax.rem(lax.axis_index("gx"), 2)
    for part in range(2):
        out[1, part] = object_field[1, part] - total2[part] * scale[...]
        for received, base in ((first1, (1 - odd_x) * half), (second1, odd_x * half)):
            at = pl.ds(pl.multiple_of(base, half), half)
            total = centre1[part, :, at] + received[part]
            out[0, part, :, at] = object_field[0, part, :, at] - total * scale[:, at]


VMEM = pl.BlockSpec(memory_space=pltpu.VMEM)
SMEM = pl.BlockSpec(memory_space=pltpu.SMEM)
HBM = pl.BlockSpec(memory_space=pltpu.HBM)


def call(body, outs, in_specs, args, scratch=(), micros=0.0, name=None):
    return pl.pallas_call(
        body,
        out_shape=[jax.ShapeDtypeStruct(shape, F32) for shape in outs],
        in_specs=in_specs,
        out_specs=[VMEM] * len(outs),
        scratch_shapes=list(scratch),
        compiler_params=pltpu.CompilerParams(vmem_limit_bytes=24 * 1024 * 1024),
        cost_estimate=pl.CostEstimate(flops=int(micros * 1e9), bytes_accessed=1, transcendentals=0),
        name=name,
    )(*args)


def shards(object_field, probe, positions, residual, saved_wave):
    window = probe.shape[-1]
    half = window // 2
    count = positions.shape[0]
    size = notes_size(count)
    wave_hi, wave_lo, move_hi, move_lo = (jnp.asarray(t) for t in tables(window))
    barrier = lax.optimization_barrier

    def twice(planes):
        return pltpu.VMEM((*planes, 2 * window + 8, window), F32)

    grads = pltpu.VMEM((2, count, window, window), F32)
    fields_shape = (count, 2, window, window)

    def pieces(planes, extra=0):
        return [(planes, half + extra, 2 * window), (planes, half + extra, 2 * window), (planes, window, 2 * window)]

    def strips(planes, extra=0):
        return [(planes, window + extra, half), (planes, window + extra, half), (planes, window, window)]

    odd_x = lax.rem(lax.axis_index("gx"), 2)
    left, right = object_field[1, :, :, :half], object_field[1, :, :, half:]
    first0 = jnp.where(odd_x == 1, left, right)
    second0 = jnp.where(odd_x == 1, right, left)
    halo_first = swapped(first0, "gx", 0)
    halo_second = swapped(second0, "gx", 1)

    field, up2, down2, middle2 = call(
        detect,
        [fields_shape] + pieces(2, size),
        [SMEM] + [VMEM] * 4,
        (positions, residual, saved_wave, wave_hi, wave_lo),
        [twice((count, 2)), grads],
        micros=12.0, name="detect",
    )
    from_up2 = swapped(up2, "gy", 0)
    from_down2 = swapped(down2, "gy", 1)

    halo_first, halo_second, field = barrier((halo_first, halo_second, field))
    fields, probes = call(
        roll_fields,
        [fields_shape] * 2,
        [SMEM] + [VMEM] * 2,
        (positions, field, probe),
        [twice((count + 1, 2))],
        micros=12.0, name="roll",
    )

    halo_first, halo_second, fields, probes, from_up2, from_down2 = barrier(
        (halo_first, halo_second, fields, probes, from_up2, from_down2)
    )
    up0, down0, wide0 = call(
        widen,
        pieces(2),
        [VMEM] * 3,
        (object_field, halo_first, halo_second),
        micros=0.2, name="widen",
    )
    from_up0 = swapped(up0, "gy", 0)
    from_down0 = swapped(down0, "gy", 1)

    first2, second2, centre2 = call(
        narrow,
        strips(2, 3 * size),
        [SMEM] + [VMEM] * 3,
        (positions, middle2, from_up2, from_down2),
        micros=0.2, name="narrow2",
    )
    from_up0, from_down0, first2, second2, centre2 = barrier((from_up0, from_down0, first2, second2, centre2))
    got_first2 = swapped(first2, "gx", 0)
    got_second2 = swapped(second2, "gx", 1)

    up1, down1, middle1 = call(
        propagate,
        pieces(2),
        [SMEM] + [VMEM] * 7,
        (positions, fields, probes, wide0, from_up0, from_down0, move_hi, move_lo),
        [pltpu.VMEM(fields_shape, BF16)] * 2 + [grads],
        micros=12.0, name="propagate",
    )
    from_up1 = swapped(up1, "gy", 0)
    from_down1 = swapped(down1, "gy", 1)
    (total2,) = call(
        join, [centre2.shape], [VMEM] * 3, (centre2, got_first2, got_second2), micros=12.0, name="join2"
    )
    middle1, total2 = barrier((middle1, total2))
    first1, second1, centre1 = call(
        narrow,
        strips(2),
        [SMEM] + [VMEM] * 3,
        (positions, middle1, from_up1, from_down1),
        micros=0.2, name="narrow1",
    )
    got_first1 = swapped(first1, "gx", 0)
    got_second1 = swapped(second1, "gx", 1)

    (scale,) = call(
        illuminate,
        [(window, window)],
        [SMEM] + [VMEM] * 5,
        (positions, probe, from_up2, from_down2, got_first2, got_second2),
        [twice(()), pltpu.SMEM((8 * size, half), F32), pltpu.SemaphoreType.DMA((4,))],
        micros=2.0, name="illuminate",
    )
    (new_object,) = call(
        update,
        [object_field.shape],
        [VMEM] * 6,
        (object_field, scale, total2, centre1, got_first1, got_second1),
        micros=1.0, name="update",
    )
    return new_object


def solution(mesh):
    placed = (
        P(None, None, "gy", "gx"),
        P(),
        P("gy", "gx", None),
        P("gy", "gx", None, None, None),
        P("gy", "gx", None, None, None),
    )
    return jax.shard_map(
        shards, mesh=mesh, in_specs=placed, out_specs=P(None, None, "gy", "gx"), check_vma=False
    )
```

```python
import functools

import jax
import jax.numpy as jnp
import ml_dtypes
import numpy as np
from jax import lax
from jax.experimental import pallas as pl
from jax.experimental.pallas import tpu as pltpu
from jax.sharding import PartitionSpec as P

fresnel_rate = 200.0
ridge = 0.5
CHUNK = 32
F32 = jnp.float32
BF16 = jnp.bfloat16


def two_parts(table):
    high = table.astype(np.float32).astype(ml_dtypes.bfloat16)
    low = (table - high.astype(np.float64)).astype(ml_dtypes.bfloat16)
    return high, low


@functools.lru_cache(maxsize=None)
def tables(size):
    index = np.arange(size)
    inverse = np.exp(2j * np.pi * (np.outer(index, index) % size) / size) / np.sqrt(size)
    freq = ((index + size // 2) % size - size // 2) / size
    move = inverse @ np.diag(np.exp(1j * fresnel_rate * freq**2)) @ inverse.conj()
    out = []
    for matrix in (inverse, move):
        out.extend(two_parts(np.concatenate([matrix.real, matrix.imag], axis=1)))
    return np.stack(out)


def swap_pairs(count, first):
    pairs = []
    for low in range(first, count - 1, 2):
        pairs += [(low, low + 1), (low + 1, low)]
    return pairs


def swapped(value, axis, first):
    return lax.ppermute(value, axis, swap_pairs(lax.axis_size(axis), first))


def dot(a, b):
    return jnp.dot(a, b, preferred_element_type=F32)


def split(value):
    high = value.astype(BF16)
    return high, (value - high.astype(F32)).astype(BF16)


def place(waves, corners, out_first, out_second, out_middle, odd, window):
    half = window // 2

    def rows(base, lower, store):
        for start in range(0, half, CHUNK):
            at = pl.multiple_of(base + start, CHUNK)
            row = lax.broadcasted_iota(jnp.int32, (CHUNK, window), 0) + at
            col = lax.broadcasted_iota(jnp.int32, (CHUNK, window), 1)
            masks = []
            for r, c in corners:
                inside = (row < r) == (lower == 1)
                masks.append((inside & (col >= c), inside & (col < c)))
            for plane in range(len(waves)):
                left = right = None
                for number, (in_left, in_right) in enumerate(masks):
                    value = waves[plane][number, pl.ds(at, CHUNK), :]
                    a = jnp.where(in_left, value, 0.0)
                    b = jnp.where(in_right, value, 0.0)
                    left = a if left is None else left + a
                    right = b if right is None else right + b
                store(plane, start, left, right)

    def writer(ref, offset):
        def store(plane, start, left, right):
            at = slice(offset + start, offset + start + CHUNK)
            if isinstance(ref, tuple):
                ref[0][plane, at, :half] = left[:, :half]
                ref[0][plane, at, half:] = right[:, half:]
                ref[1][plane, at, :half] = left[:, half:]
                ref[1][plane, at, half:] = right[:, :half]
            else:
                ref[plane, at, :window] = left
                ref[plane, at, window:] = right

        return store

    rows((1 - odd) * half, 1 - odd, writer(out_first, 0))
    rows(odd * half, odd, writer(out_second, 0))
    rows(half, 0, writer(out_middle, 0))
    rows(0, 1, writer(out_middle, half))


def from_right(rows_re, rows_im, high, low, passes):
    window = high.shape[0]
    sums = []
    for rows in (rows_re, rows_im):
        total = dot(rows[0], high[...]) + dot(rows[0], low[...])
        if passes == 3:
            total += dot(rows[1], high[...])
        sums.append(total)
    one, two = sums
    return one[:, :window] - two[:, window:], one[:, window:] + two[:, :window]


def from_left(high, low, inner_hi, inner_lo):
    window = high.shape[0]
    sums = []
    for part in range(2):
        cols = slice(part * window, (part + 1) * window)
        sums.append(dot(high[:, cols], inner_hi) + dot(low[:, cols], inner_hi) + dot(high[:, cols], inner_lo))
    one, two = sums
    return one[:, :window] - two[:, window:], one[:, window:] + two[:, :window]


def rolled(twice, corner, store, window):
    r, c = corner
    rest = lax.rem(window - r, 8)
    back = lax.rem(CHUNK + 8 - rest, CHUNK + 8)
    for start in range(0, window, CHUNK):
        value = twice[pl.ds(pl.multiple_of(window - r - rest + start, 8), CHUNK + 8), :]
        store(start, pltpu.roll(pltpu.roll(value, back, 0)[:CHUNK], c, 1))


def twofold(twice, start, value, window):
    rows = value.shape[0]
    twice[start : start + rows] = value
    twice[window + start : window + start + rows] = value
    if start == 0:
        twice[2 * window : 2 * window + 8] = value[:8]


def corners_of(pos):
    return [(pos[number, 0, 0], pos[number, 0, 1]) for number in range(pos.shape[0])]


def fetched(pos_any, pos, sem):
    copy = pltpu.make_async_copy(pos_any, pos, sem)
    copy.start()
    return copy


def detect(
    pos_any, residual, wave, table, field, first, second, middle, notes, marks, twice, grads, pos, sem
):
    window = residual.shape[-1]
    count = residual.shape[0]
    odd = lax.rem(lax.axis_index("gy"), 2)
    arrival = fetched(pos_any, pos, sem)
    table_hi, table_lo = table.at[0], table.at[1]
    for number in range(count):
        line = from_right((residual[number, 0, 0],), (residual[number, 0, 1],), table_hi, table_lo, 2)
        high, low = split(jnp.concatenate(line, axis=1))
        field_re, field_im = from_left(table_hi, table_lo, high, low)
        field[number, 0] = field_re
        field[number, 1] = field_im
        for start in range(0, window, CHUNK):
            rows = slice(start, start + CHUNK)
            wave_re, wave_im = wave[number, 0, 0, rows].astype(F32), wave[number, 0, 1, rows].astype(F32)
            value_re, value_im = field[number, 0, rows], field[number, 1, rows]
            twofold(twice.at[number, 0], start, wave_re * value_re + wave_im * value_im, window)
            twofold(twice.at[number, 1], start, wave_re * value_im - wave_im * value_re, window)
    arrival.wait()
    corners = corners_of(pos)
    for number, corner in enumerate(corners):
        for part in range(2):

            def store(start, value):
                grads[part, number, start : start + CHUNK] = value

            rolled(twice.at[number, part], corner, store, window)
            marks[2 * number + part] = jnp.full(marks.shape[1:], corner[part], jnp.int32)
    place([grads.at[0], grads.at[1]], corners, first, second, middle, odd, window)
    for ref in (first, second):
        ref[0, window // 2 :] = notes_of(pos, count, 2 * window)
    notes[...] = notes_of(pos, count, window // 2)


def roll_fields(pos_any, field, probe, field_out, probes, twice, pos, sem):
    window = probe.shape[-1]
    count = field.shape[0]
    arrival = fetched(pos_any, pos, sem)
    for part in range(2):
        for start in range(0, window, CHUNK):
            twofold(twice.at[count, part], start, probe[part, start : start + CHUNK], window)
            for number in range(count):
                twofold(twice.at[number, part], start, field[number, part, start : start + CHUNK], window)
    arrival.wait()
    for number, corner in enumerate(corners_of(pos)):
        for part in range(2):

            def to_field(start, value):
                field_out[number, part, start : start + CHUNK] = value

            rolled(twice.at[number, part], corner, to_field, window)

            def to_probes(start, value):
                probes[number, part, start : start + CHUNK] = value

            rolled(twice.at[count, part], corner, to_probes, window)


def notes_size(count):
    return -(-(1 + 2 * count) // 8) * 8


def notes_of(pos, count, width):
    size = notes_size(count)
    row = lax.broadcasted_iota(jnp.int32, (size, width), 0)
    notes = jnp.where(row == 0, 1, 0)
    for number in range(count):
        for part in range(2):
            notes = jnp.where(row == 1 + 2 * number + part, pos[number, 0, part], notes)
    return notes.astype(F32)


def sides(odd, one, two):
    return jnp.where(odd == 1, one, two), jnp.where(odd == 1, two, one)


def edges(object_field, first, second, own_first, own_second):
    window = object_field.shape[-1]
    half = window // 2
    odd_x = lax.rem(lax.axis_index("gx"), 2)
    odd_y = lax.rem(lax.axis_index("gy"), 2)
    for ref, odd in ((first, 1 - odd_x), (second, odd_x)):
        ref[...] = object_field[1, :, :, pl.ds(pl.multiple_of(odd * half, half), half)]
    for ref, odd in ((own_first, 1 - odd_y), (own_second, odd_y)):
        ref[...] = object_field[1, :, pl.ds(pl.multiple_of(odd * half, half), half), :]


def relay(from_first, from_second, first, second):
    half = from_first.shape[-1]
    odd_x = lax.rem(lax.axis_index("gx"), 2)
    odd_y = lax.rem(lax.axis_index("gy"), 2)
    at_first = pl.ds(pl.multiple_of((1 - odd_x) * half, half), half)
    at_second = pl.ds(pl.multiple_of(odd_x * half, half), half)
    for ref, base in ((first, (1 - odd_y) * half), (second, odd_y * half)):
        rows = pl.ds(pl.multiple_of(base, half), half)
        for plane in range(ref.shape[0]):
            ref[plane, :, at_first] = from_first[plane, rows]
            ref[plane, :, at_second] = from_second[plane, rows]


def propagate(
    marks, field, probes, object_field, halo_first, halo_second,
    own_first, own_second, corner_first, corner_second, table,
    outer_first, outer_second, inner_first, inner_second, middle,
    chi_hi, chi_lo, grads,
):
    window = field.shape[-1]
    half = window // 2
    count = field.shape[0]
    odd_x = lax.rem(lax.axis_index("gx"), 2)
    odd = lax.rem(lax.axis_index("gy"), 2)
    corners = [(marks[2 * number, :1], marks[2 * number + 1, :1]) for number in range(count)]
    table_hi, table_lo = table.at[2], table.at[3]

    def wide(part, rows):
        left, right = sides(odd_x, halo_first[part, rows], halo_second[part, rows])
        return jnp.concatenate([left, object_field[1, part, rows], right], axis=1)

    def beyond(part, rows, below):
        own = sides(odd, own_first[part, rows], own_second[part, rows])[below]
        corner = sides(odd, corner_first[part, rows], corner_second[part, rows])[below]
        return jnp.concatenate([corner[:, :half], own, corner[:, half:]], axis=1)

    for start in range(0, window, CHUNK):
        rows = slice(start, start + CHUNK)
        row = lax.broadcasted_iota(jnp.int32, (CHUNK, window), 0) + start
        col = lax.broadcasted_iota(jnp.int32, (CHUNK, window), 1)
        upper, lower = [], []
        for part in range(2):
            if start < half:
                upper.append(beyond(part, rows, 0))
                lower.append(wide(part, slice(half + start, half + start + CHUNK)))
            else:
                shifted = slice(start - half, start - half + CHUNK)
                upper.append(wide(part, shifted))
                lower.append(beyond(part, shifted, 1))
        for number, (r, c) in enumerate(corners):
            low_row, low_col = row < r, col < c
            patch = []
            for part in range(2):
                above = jnp.where(low_col, upper[part][:, window:], upper[part][:, :window])
                below = jnp.where(low_col, lower[part][:, window:], lower[part][:, :window])
                patch.append(jnp.where(low_row, below, above))
            field_re, field_im = field[number, 0, rows], field[number, 1, rows]
            high, low = split(patch[0] * field_re + patch[1] * field_im)
            chi_hi[number, 0, rows] = high
            chi_lo[number, 0, rows] = low
            high, low = split(patch[0] * field_im - patch[1] * field_re)
            chi_hi[number, 1, rows] = high
            chi_lo[number, 1, rows] = low

    for number in range(count):
        line = from_right(
            (chi_hi[number, 0], chi_lo[number, 0]), (chi_hi[number, 1], chi_lo[number, 1]), table_hi, table_lo, 3
        )
        high, low = split(jnp.concatenate(line, axis=1))
        back_re, back_im = from_left(table_hi, table_lo, high, low)
        probe_re, probe_im = probes[number, 0], probes[number, 1]
        grads[0, number] = probe_re * back_re + probe_im * back_im
        grads[1, number] = probe_re * back_im - probe_im * back_re
    place(
        [grads.at[0], grads.at[1]], corners, (outer_first, inner_first), (outer_second, inner_second), middle, odd, window
    )


def illuminate(pos, probe, up, down, first, second, scale, twice, notes, sems):
    window = probe.shape[-1]
    half = window // 2
    count = pos.shape[0]
    size = notes_size(count)
    odd_x = lax.rem(lax.axis_index("gx"), 2)
    odd_y = lax.rem(lax.axis_index("gy"), 2)
    copies, at = [], 0
    for ref, start, rows in ((up, half, size), (down, half, size), (first, window, 3 * size), (second, window, 3 * size)):
        source = ref.at[0, pl.ds(start, rows), pl.ds(0, half)]
        copies.append(pltpu.make_async_copy(source, notes.at[pl.ds(at, rows), :], sems.at[len(copies)]))
        copies[-1].start()
        at += rows
    for start in range(0, window, CHUNK):
        rows = slice(start, start + CHUNK)
        twofold(twice, start, probe[0, rows] * probe[0, rows] + probe[1, rows] * probe[1, rows], window)
    for copy in copies:
        copy.wait()

    shifts = []
    for down in (-1, 0, 1):
        for along in (-1, 0, 1):
            if along == 0:
                base = (odd_y if down > 0 else 1 - odd_y) * size
            else:
                base = (2 + 3 * (odd_x if along > 0 else 1 - odd_x) + 1 + down) * size
            for number in range(count):
                if down == 0 and along == 0:
                    valid, r, c = 1, pos[number, 0, 0], pos[number, 0, 1]
                else:
                    valid, r, c = (
                        notes[base + row, 0].astype(jnp.int32) for row in (0, 1 + 2 * number, 2 + 2 * number)
                    )
                top = r - half + window * down
                left = c - half + window * along
                top = jnp.where(valid == 1, top, window)
                shifts.append((top, left, r, c))

    def rows_at(index, carry):
        start = index * CHUNK
        row = lax.broadcasted_iota(jnp.int32, (CHUNK, window), 0) + start
        col = lax.broadcasted_iota(jnp.int32, (CHUNK, window), 1)
        total = jnp.zeros((CHUNK, window), F32)
        for top, left, r, c in shifts:
            turn = lax.rem(2 * window - half - r, window)
            rest = lax.rem(turn, 8)
            value = twice[pl.ds(pl.multiple_of(turn - rest + start, 8), CHUNK + 8), :]
            value = pltpu.roll(value, lax.rem(CHUNK + 8 - rest, CHUNK + 8), 0)[:CHUNK]
            value = pltpu.roll(value, lax.rem(c + half, window), 1)
            inside = (row >= top) & (row < top + window) & (col >= left) & (col < left + window)
            total += jnp.where(inside, value, 0.0)
        scale[pl.ds(pl.multiple_of(start, CHUNK), CHUNK), :] = 1.0 / (total + ridge)
        return carry

    lax.fori_loop(0, window // CHUNK, rows_at, 0)


def narrow(notes, middle, from_first, from_second, first, second, centre):
    half = first.shape[-1]
    window = 2 * half
    odd_x = lax.rem(lax.axis_index("gx"), 2)
    odd_y = lax.rem(lax.axis_index("gy"), 2)
    for plane in range(middle.shape[0]):
        for start in range(0, half, CHUNK):
            rows = slice(start, start + CHUNK)
            for received, base in ((from_first, (1 - odd_y) * half), (from_second, odd_y * half)):
                at = pl.ds(pl.multiple_of(base + start, CHUNK), CHUNK)
                total = middle[plane, at, :] + received[plane, rows]
                centre[plane, at, :] = total[:, half : 3 * half]
                second[plane, at, :], first[plane, at, :] = sides(odd_x, total[:, 3 * half :], total[:, :half])
    size = notes.shape[0]
    above, below = sides(odd_y, from_first[0, half:, :half], from_second[0, half:, :half])
    for ref in (first, second):
        ref[0, window : window + size] = above
        ref[0, window + size : window + 2 * size] = notes[...]
        ref[0, window + 2 * size :] = below


def narrow_outer(middle, from_first, from_second, first, second):
    half = first.shape[-1]
    odd_x = lax.rem(lax.axis_index("gx"), 2)
    odd_y = lax.rem(lax.axis_index("gy"), 2)
    for plane in range(middle.shape[0]):
        for received, base in ((from_first, (1 - odd_y) * half), (from_second, odd_y * half)):
            at = pl.ds(pl.multiple_of(base, half), half)
            left = middle[plane, at, :half] + received[plane, :, :half]
            right = middle[plane, at, 3 * half :] + received[plane, :, half:]
            second[plane, at, :], first[plane, at, :] = sides(odd_x, right, left)


def join(centre, from_first, from_second, out):
    window = centre.shape[-1]
    half = window // 2
    odd_x = lax.rem(lax.axis_index("gx"), 2)
    for plane in range(centre.shape[0]):
        for received, base in ((from_first, (1 - odd_x) * half), (from_second, odd_x * half)):
            at = pl.ds(pl.multiple_of(base, half), half)
            out[plane, :, at] = centre[plane, :, at] + received[plane, :window]


def update(first1, second1, object_field, scale, total2, middle1, inner_first, inner_second, out):
    window = scale.shape[-1]
    half = window // 2
    odd_x = lax.rem(lax.axis_index("gx"), 2)
    odd_y = lax.rem(lax.axis_index("gy"), 2)
    for part in range(2):
        out[1, part] = object_field[1, part] - total2[part] * scale[...]
        for received, base in ((inner_first, (1 - odd_y) * half), (inner_second, odd_y * half)):
            rows = pl.ds(pl.multiple_of(base, half), half)
            outer = jnp.concatenate(sides(odd_x, first1[part, rows], second1[part, rows]), axis=1)
            total = middle1[part, rows, half : 3 * half] + received[part] + outer
            out[0, part, rows] = object_field[0, part, rows] - total * scale[rows]


VMEM = pl.BlockSpec(memory_space=pltpu.VMEM)
SMEM = pl.BlockSpec(memory_space=pltpu.SMEM)
ANY = pl.BlockSpec(memory_space=pl.ANY)


def call(body, outs, in_specs, args, scratch=(), micros=0.0, name=None):
    return pl.pallas_call(
        body,
        out_shape=[x if hasattr(x, "dtype") else jax.ShapeDtypeStruct(x, F32) for x in outs],
        in_specs=in_specs,
        out_specs=[VMEM] * len(outs),
        scratch_shapes=list(scratch),
        compiler_params=pltpu.CompilerParams(vmem_limit_bytes=24 * 1024 * 1024),
        cost_estimate=pl.CostEstimate(flops=int(micros * 1e9), bytes_accessed=1, transcendentals=0),
        name=name,
    )(*args)


def shards(object_field, probe, positions, residual, saved_wave):
    window = probe.shape[-1]
    half = window // 2
    count = positions.shape[0]
    size = notes_size(count)
    table = jnp.asarray(tables(window))
    barrier = lax.optimization_barrier

    def twice(*planes):
        return pltpu.VMEM((*planes, 2 * window + 8, window), F32)

    grads = pltpu.VMEM((2, count, window, window), F32)
    pos_scratch = [pltpu.SMEM(positions.shape, jnp.int32), pltpu.SemaphoreType.DMA]
    fields_shape = (count, 2, window, window)
    wide_shape = (2, window, 2 * window)
    square, strip = (2, half, window), (2, window, half)

    edge_first, edge_second, rows_first, rows_second = call(
        edges, [strip] * 2 + [square] * 2, [VMEM], (object_field,), micros=0.2, name="edges"
    )
    halo_first = swapped(edge_first, "gx", 0)
    halo_second = swapped(edge_second, "gx", 1)

    field, up2, down2, middle2, notes, marks = call(
        detect,
        [fields_shape]
        + [(2, half + size, 2 * window)] * 2
        + [wide_shape, (size, half), jax.ShapeDtypeStruct((2 * count, 8, window), jnp.int32)],
        [ANY] + [VMEM] * 3,
        (positions, residual, saved_wave, table),
        [twice(count, 2), grads] + pos_scratch,
        micros=12.0, name="detect",
    )
    up2, down2, rows_first, rows_second = barrier((up2, down2, rows_first, rows_second))
    from_up2 = swapped(up2, "gy", 0)
    from_down2 = swapped(down2, "gy", 1)
    own_first = swapped(rows_first, "gy", 0)
    own_second = swapped(rows_second, "gy", 1)

    fields, probes = call(
        roll_fields,
        [fields_shape] * 2,
        [ANY] + [VMEM] * 2,
        (positions, field, probe),
        [twice(count + 1, 2)] + pos_scratch,
        micros=0.1, name="roll",
    )
    corner0_first, corner0_second = call(
        relay, [square] * 2, [VMEM] * 2, (halo_first, halo_second), micros=12.0, name="widen"
    )
    from_corner0_first = swapped(corner0_first, "gy", 0)
    from_corner0_second = swapped(corner0_second, "gy", 1)

    from_up2, from_down2, own_first, own_second, fields, probes = barrier(
        (from_up2, from_down2, own_first, own_second, fields, probes)
    )
    first2, second2, centre2 = call(
        narrow,
        [(2, window + 3 * size, half)] * 2 + [fields_shape[1:]],
        [VMEM] * 4,
        (notes, middle2, from_up2, from_down2),
        micros=0.2, name="narrow2",
    )
    from_corner0_first, from_corner0_second, first2, second2, centre2 = barrier(
        (from_corner0_first, from_corner0_second, first2, second2, centre2)
    )
    got_first2 = swapped(first2, "gx", 0)
    got_second2 = swapped(second2, "gx", 1)

    outer_first, outer_second, inner_first, inner_second, middle1 = call(
        propagate,
        [square] * 4 + [wide_shape],
        [VMEM] * 11,
        (marks, fields, probes, object_field, halo_first, halo_second, own_first, own_second)
        + (from_corner0_first, from_corner0_second, table),
        [pltpu.VMEM(fields_shape, BF16)] * 2 + [grads],
        micros=0.1, name="propagate",
    )
    from_outer_first = swapped(outer_first, "gy", 0)
    from_outer_second = swapped(outer_second, "gy", 1)
    (total2,) = call(join, [centre2.shape], [VMEM] * 3, (centre2, got_first2, got_second2), micros=12.0, name="join2")
    first1, second1 = call(
        narrow_outer, [strip] * 2, [VMEM] * 3, (middle1, from_outer_first, from_outer_second), micros=0.2, name="narrow1"
    )
    first1, second1, inner_first, inner_second = barrier((first1, second1, inner_first, inner_second))
    got_first1 = swapped(first1, "gx", 0)
    got_second1 = swapped(second1, "gx", 1)
    from_inner_first = swapped(inner_first, "gy", 0)
    from_inner_second = swapped(inner_second, "gy", 1)

    (scale,) = call(
        illuminate,
        [(window, window)],
        [SMEM] + [VMEM] * 5,
        (positions, probe, from_up2, from_down2, got_first2, got_second2),
        [twice(), pltpu.SMEM((8 * size, half), F32), pltpu.SemaphoreType.DMA((4,))],
        micros=12.0, name="illuminate",
    )
    (new_object,) = call(
        update,
        [object_field.shape],
        [VMEM] * 8,
        (got_first1, got_second1, object_field, scale, total2, middle1, from_inner_first, from_inner_second),
        micros=1.0, name="update",
    )
    return new_object


def solution(mesh):
    placed = (
        P(None, None, "gy", "gx"),
        P(),
        P("gy", "gx", None),
        P("gy", "gx", None, None, None),
        P("gy", "gx", None, None, None),
    )
    return jax.shard_map(
        shards, mesh=mesh, in_specs=placed, out_specs=P(None, None, "gy", "gx"), check_vma=False
    )
```

```python
import functools

import jax
import jax.numpy as jnp
import ml_dtypes
import numpy as np
from jax import lax
from jax.experimental import pallas as pl
from jax.experimental.pallas import tpu as pltpu
from jax.sharding import PartitionSpec as P

fresnel_rate = 200.0
ridge = 0.5
CHUNK = 32
F32 = jnp.float32
BF16 = jnp.bfloat16


def two_parts(table):
    high = table.astype(np.float32).astype(ml_dtypes.bfloat16)
    low = (table - high.astype(np.float64)).astype(ml_dtypes.bfloat16)
    return high, low


@functools.lru_cache(maxsize=None)
def tables(size):
    index = np.arange(size)
    inverse = np.exp(2j * np.pi * (np.outer(index, index) % size) / size) / np.sqrt(size)
    freq = ((index + size // 2) % size - size // 2) / size
    move = inverse @ np.diag(np.exp(1j * fresnel_rate * freq**2)) @ inverse.conj()
    out = []
    for matrix in (inverse, move):
        out.extend(two_parts(np.concatenate([matrix.real, matrix.imag], axis=1)))
    return np.stack(out)


def swap_pairs(count, first):
    pairs = []
    for low in range(first, count - 1, 2):
        pairs += [(low, low + 1), (low + 1, low)]
    return pairs


def swapped(value, axis, first):
    return lax.ppermute(value, axis, swap_pairs(lax.axis_size(axis), first))


def dot(a, b):
    return jnp.dot(a, b, preferred_element_type=F32)


def split(value):
    high = value.astype(BF16)
    return high, (value - high.astype(F32)).astype(BF16)


def place(waves, corners, out_first, out_second, out_middle, odd, window):
    half = window // 2

    def rows(base, lower, store):
        for start in range(0, half, CHUNK):
            at = pl.multiple_of(base + start, CHUNK)
            row = lax.broadcasted_iota(jnp.int32, (CHUNK, window), 0) + at
            col = lax.broadcasted_iota(jnp.int32, (CHUNK, window), 1)
            masks = []
            for r, c in corners:
                inside = (row < r) == (lower == 1)
                masks.append((inside & (col >= c), inside & (col < c)))
            for plane in range(len(waves)):
                left = right = None
                for number, (in_left, in_right) in enumerate(masks):
                    value = waves[plane][number, pl.ds(at, CHUNK), :]
                    a = jnp.where(in_left, value, 0.0)
                    b = jnp.where(in_right, value, 0.0)
                    left = a if left is None else left + a
                    right = b if right is None else right + b
                store(plane, start, left, right)

    def writer(ref, offset):
        def store(plane, start, left, right):
            at = slice(offset + start, offset + start + CHUNK)
            if isinstance(ref, tuple):
                ref[0][plane, at, :half] = left[:, :half]
                ref[0][plane, at, half:] = right[:, half:]
                ref[1][plane, at, :half] = left[:, half:]
                ref[1][plane, at, half:] = right[:, :half]
            else:
                ref[plane, at, :window] = left
                ref[plane, at, window:] = right

        return store

    rows((1 - odd) * half, 1 - odd, writer(out_first, 0))
    rows(odd * half, odd, writer(out_second, 0))
    rows(half, 0, writer(out_middle, 0))
    rows(0, 1, writer(out_middle, half))


def from_right(rows_re, rows_im, high, low, passes):
    window = high.shape[0]
    sums = []
    for rows in (rows_re, rows_im):
        total = dot(rows[0], high[...]) + dot(rows[0], low[...])
        if passes == 3:
            total += dot(rows[1], high[...])
        sums.append(total)
    one, two = sums
    return one[:, :window] - two[:, window:], one[:, window:] + two[:, :window]


def from_left(high, low, inner_hi, inner_lo):
    window = high.shape[0]
    sums = []
    for part in range(2):
        cols = slice(part * window, (part + 1) * window)
        sums.append(dot(high[:, cols], inner_hi) + dot(low[:, cols], inner_hi) + dot(high[:, cols], inner_lo))
    one, two = sums
    return one[:, :window] - two[:, window:], one[:, window:] + two[:, :window]


def rolled(twice, corner, store, window):
    r, c = corner
    rest = lax.rem(window - r, 8)
    back = lax.rem(CHUNK + 8 - rest, CHUNK + 8)
    for start in range(0, window, CHUNK):
        value = twice[pl.ds(pl.multiple_of(window - r - rest + start, 8), CHUNK + 8), :]
        store(start, pltpu.roll(pltpu.roll(value, back, 0)[:CHUNK], c, 1))


def twofold(twice, start, value, window):
    rows = value.shape[0]
    twice[start : start + rows] = value
    twice[window + start : window + start + rows] = value
    if start == 0:
        twice[2 * window : 2 * window + 8] = value[:8]


def corners_of(pos):
    return [(pos[number, 0, 0], pos[number, 0, 1]) for number in range(pos.shape[0])]


def fetched(pos_any, pos, sem):
    copy = pltpu.make_async_copy(pos_any, pos, sem)
    copy.start()
    return copy


def detect(
    pos_any, residual, wave, table,
    field, first, second, middle, notes, marks,
    twice, grads, pos, sem,
):
    window = residual.shape[-1]
    count = residual.shape[0]
    odd = lax.rem(lax.axis_index("gy"), 2)
    arrival = fetched(pos_any, pos, sem)
    table_hi, table_lo = table.at[0], table.at[1]
    for number in range(count):
        line = from_right((residual[number, 0, 0],), (residual[number, 0, 1],), table_hi, table_lo, 2)
        high, low = split(jnp.concatenate(line, axis=1))
        field_re, field_im = from_left(table_hi, table_lo, high, low)
        field[number, 0] = field_re
        field[number, 1] = field_im
        for start in range(0, window, CHUNK):
            rows = slice(start, start + CHUNK)
            wave_re, wave_im = wave[number, 0, 0, rows].astype(F32), wave[number, 0, 1, rows].astype(F32)
            value_re, value_im = field[number, 0, rows], field[number, 1, rows]
            twofold(twice.at[number, 0], start, wave_re * value_re + wave_im * value_im, window)
            twofold(twice.at[number, 1], start, wave_re * value_im - wave_im * value_re, window)
    arrival.wait()
    corners = corners_of(pos)
    for number, corner in enumerate(corners):
        for part in range(2):

            def store(start, value):
                grads[part, number, start : start + CHUNK] = value

            rolled(twice.at[number, part], corner, store, window)
            marks[2 * number + part] = jnp.full(marks.shape[1:], corner[part], jnp.int32)
    place([grads.at[0], grads.at[1]], corners, first, second, middle, odd, window)
    for ref in (first, second):
        ref[0, window // 2 :] = notes_of(pos, count, 2 * window)
    notes[...] = notes_of(pos, count, window // 2)


def roll_fields(pos_any, field, probe, field_out, probes, twice, pos, sem):
    window = probe.shape[-1]
    count = field.shape[0]
    arrival = fetched(pos_any, pos, sem)
    for part in range(2):
        for start in range(0, window, CHUNK):
            twofold(twice.at[count, part], start, probe[part, start : start + CHUNK], window)
            for number in range(count):
                twofold(twice.at[number, part], start, field[number, part, start : start + CHUNK], window)
    arrival.wait()
    for number, corner in enumerate(corners_of(pos)):
        for part in range(2):

            def to_field(start, value):
                field_out[number, part, start : start + CHUNK] = value

            rolled(twice.at[number, part], corner, to_field, window)

            def to_probes(start, value):
                probes[number, part, start : start + CHUNK] = value

            rolled(twice.at[count, part], corner, to_probes, window)


def notes_size(count):
    return -(-(1 + 2 * count) // 8) * 8


def notes_of(pos, count, width):
    size = notes_size(count)
    row = lax.broadcasted_iota(jnp.int32, (size, width), 0)
    notes = jnp.where(row == 0, 1, 0)
    for number in range(count):
        for part in range(2):
            notes = jnp.where(row == 1 + 2 * number + part, pos[number, 0, part], notes)
    return notes.astype(F32)


def sides(odd, one, two):
    return jnp.where(odd == 1, one, two), jnp.where(odd == 1, two, one)


def edges(object_field, first, second):
    half = object_field.shape[-1] // 2
    odd_x = lax.rem(lax.axis_index("gx"), 2)
    for ref, odd in ((first, 1 - odd_x), (second, odd_x)):
        ref[...] = object_field[1, :, :, pl.ds(pl.multiple_of(odd * half, half), half)]


def relay(object_field, from_first, from_second, first, second):
    half = from_first.shape[-1]
    odd_x = lax.rem(lax.axis_index("gx"), 2)
    odd_y = lax.rem(lax.axis_index("gy"), 2)
    at_first = pl.ds(pl.multiple_of((1 - odd_x) * 3 * half, half), half)
    at_second = pl.ds(pl.multiple_of(odd_x * 3 * half, half), half)
    for ref, base in ((first, (1 - odd_y) * half), (second, odd_y * half)):
        rows = pl.ds(pl.multiple_of(base, half), half)
        for plane in range(ref.shape[0]):
            ref[plane, :, half : 3 * half] = object_field[1, plane, rows]
            ref[plane, :, at_first] = from_first[plane, rows]
            ref[plane, :, at_second] = from_second[plane, rows]


def propagate(
    marks, field, probes, object_field, halo_first, halo_second,
    rows_first, rows_second, table,
    outer_first, outer_second, inner_first, inner_second, middle,
    chi_hi, chi_lo, grads,
):
    window = field.shape[-1]
    half = window // 2
    count = field.shape[0]
    odd_x = lax.rem(lax.axis_index("gx"), 2)
    odd = lax.rem(lax.axis_index("gy"), 2)
    corners = [(marks[2 * number, :1], marks[2 * number + 1, :1]) for number in range(count)]
    table_hi, table_lo = table.at[2], table.at[3]

    def wide(part, rows):
        left, right = sides(odd_x, halo_first[part, rows], halo_second[part, rows])
        return jnp.concatenate([left, object_field[1, part, rows], right], axis=1)

    def beyond(part, rows, below):
        return sides(odd, rows_first[part, rows], rows_second[part, rows])[below]

    for start in range(0, window, CHUNK):
        rows = slice(start, start + CHUNK)
        row = lax.broadcasted_iota(jnp.int32, (CHUNK, window), 0) + start
        col = lax.broadcasted_iota(jnp.int32, (CHUNK, window), 1)
        upper, lower = [], []
        for part in range(2):
            if start < half:
                upper.append(beyond(part, rows, 0))
                lower.append(wide(part, slice(half + start, half + start + CHUNK)))
            else:
                shifted = slice(start - half, start - half + CHUNK)
                upper.append(wide(part, shifted))
                lower.append(beyond(part, shifted, 1))
        for number, (r, c) in enumerate(corners):
            low_row, low_col = row < r, col < c
            patch = []
            for part in range(2):
                above = jnp.where(low_col, upper[part][:, window:], upper[part][:, :window])
                below = jnp.where(low_col, lower[part][:, window:], lower[part][:, :window])
                patch.append(jnp.where(low_row, below, above))
            field_re, field_im = field[number, 0, rows], field[number, 1, rows]
            high, low = split(patch[0] * field_re + patch[1] * field_im)
            chi_hi[number, 0, rows] = high
            chi_lo[number, 0, rows] = low
            high, low = split(patch[0] * field_im - patch[1] * field_re)
            chi_hi[number, 1, rows] = high
            chi_lo[number, 1, rows] = low

    for number in range(count):
        line = from_right(
            (chi_hi[number, 0], chi_lo[number, 0]), (chi_hi[number, 1], chi_lo[number, 1]), table_hi, table_lo, 3
        )
        high, low = split(jnp.concatenate(line, axis=1))
        back_re, back_im = from_left(table_hi, table_lo, high, low)
        probe_re, probe_im = probes[number, 0], probes[number, 1]
        grads[0, number] = probe_re * back_re + probe_im * back_im
        grads[1, number] = probe_re * back_im - probe_im * back_re
    place(
        [grads.at[0], grads.at[1]], corners, (outer_first, inner_first), (outer_second, inner_second), middle, odd, window
    )


def illuminate(pos, probe, up, down, first, second, scale, twice, notes, sems):
    window = probe.shape[-1]
    half = window // 2
    count = pos.shape[0]
    size = notes_size(count)
    odd_x = lax.rem(lax.axis_index("gx"), 2)
    odd_y = lax.rem(lax.axis_index("gy"), 2)
    copies, at = [], 0
    for ref, start, rows in ((up, half, size), (down, half, size), (first, window, 3 * size), (second, window, 3 * size)):
        source = ref.at[0, pl.ds(start, rows), pl.ds(0, half)]
        copies.append(pltpu.make_async_copy(source, notes.at[pl.ds(at, rows), :], sems.at[len(copies)]))
        copies[-1].start()
        at += rows
    for start in range(0, window, CHUNK):
        rows = slice(start, start + CHUNK)
        twofold(twice, start, probe[0, rows] * probe[0, rows] + probe[1, rows] * probe[1, rows], window)
    for copy in copies:
        copy.wait()

    shifts = []
    for down in (-1, 0, 1):
        for along in (-1, 0, 1):
            if along == 0:
                base = (odd_y if down > 0 else 1 - odd_y) * size
            else:
                base = (2 + 3 * (odd_x if along > 0 else 1 - odd_x) + 1 + down) * size
            for number in range(count):
                if down == 0 and along == 0:
                    valid, r, c = 1, pos[number, 0, 0], pos[number, 0, 1]
                else:
                    valid, r, c = (
                        notes[base + row, 0].astype(jnp.int32) for row in (0, 1 + 2 * number, 2 + 2 * number)
                    )
                top = r - half + window * down
                left = c - half + window * along
                top = jnp.where(valid == 1, top, window)
                shifts.append((top, left, r, c))

    def rows_at(index, carry):
        start = index * CHUNK
        row = lax.broadcasted_iota(jnp.int32, (CHUNK, window), 0) + start
        col = lax.broadcasted_iota(jnp.int32, (CHUNK, window), 1)
        total = jnp.zeros((CHUNK, window), F32)
        for top, left, r, c in shifts:
            turn = lax.rem(2 * window - half - r, window)
            rest = lax.rem(turn, 8)
            value = twice[pl.ds(pl.multiple_of(turn - rest + start, 8), CHUNK + 8), :]
            value = pltpu.roll(value, lax.rem(CHUNK + 8 - rest, CHUNK + 8), 0)[:CHUNK]
            value = pltpu.roll(value, lax.rem(c + half, window), 1)
            inside = (row >= top) & (row < top + window) & (col >= left) & (col < left + window)
            total += jnp.where(inside, value, 0.0)
        scale[pl.ds(pl.multiple_of(start, CHUNK), CHUNK), :] = 1.0 / (total + ridge)
        return carry

    lax.fori_loop(0, window // CHUNK, rows_at, 0)


def narrow(notes, middle, from_first, from_second, first, second, centre):
    half = first.shape[-1]
    window = 2 * half
    odd_x = lax.rem(lax.axis_index("gx"), 2)
    odd_y = lax.rem(lax.axis_index("gy"), 2)
    for plane in range(middle.shape[0]):
        for start in range(0, half, CHUNK):
            rows = slice(start, start + CHUNK)
            for received, base in ((from_first, (1 - odd_y) * half), (from_second, odd_y * half)):
                at = pl.ds(pl.multiple_of(base + start, CHUNK), CHUNK)
                total = middle[plane, at, :] + received[plane, rows]
                centre[plane, at, :] = total[:, half : 3 * half]
                second[plane, at, :], first[plane, at, :] = sides(odd_x, total[:, 3 * half :], total[:, :half])
    size = notes.shape[0]
    above, below = sides(odd_y, from_first[0, half:, :half], from_second[0, half:, :half])
    for ref in (first, second):
        ref[0, window : window + size] = above
        ref[0, window + size : window + 2 * size] = notes[...]
        ref[0, window + 2 * size :] = below


def narrow_outer(middle, from_first, from_second, first, second):
    half = first.shape[-1]
    odd_x = lax.rem(lax.axis_index("gx"), 2)
    odd_y = lax.rem(lax.axis_index("gy"), 2)
    for plane in range(middle.shape[0]):
        for received, base in ((from_first, (1 - odd_y) * half), (from_second, odd_y * half)):
            at = pl.ds(pl.multiple_of(base, half), half)
            left = middle[plane, at, :half] + received[plane, :, :half]
            right = middle[plane, at, 3 * half :] + received[plane, :, half:]
            second[plane, at, :], first[plane, at, :] = sides(odd_x, right, left)


def join(centre, received, out, low):
    window = centre.shape[-1]
    half = window // 2
    odd_x = lax.rem(lax.axis_index("gx"), 2)
    base = (odd_x if low else 1 - odd_x) * half
    at = pl.ds(pl.multiple_of(base, half), half)
    out[...] = centre[:, :, at] + received[:, :window]


def update(first1, second1, object_field, scale, total2_first, total2_second, middle1, inner_first, inner_second, out):
    window = scale.shape[-1]
    half = window // 2
    odd_x = lax.rem(lax.axis_index("gx"), 2)
    odd_y = lax.rem(lax.axis_index("gy"), 2)
    for part in range(2):
        total = jnp.concatenate(sides(odd_x, total2_first[part], total2_second[part]), axis=1)
        out[1, part] = object_field[1, part] - total * scale[...]
        for received, base in ((inner_first, (1 - odd_y) * half), (inner_second, odd_y * half)):
            rows = pl.ds(pl.multiple_of(base, half), half)
            outer = jnp.concatenate(sides(odd_x, first1[part, rows], second1[part, rows]), axis=1)
            total = middle1[part, rows, half : 3 * half] + received[part] + outer
            out[0, part, rows] = object_field[0, part, rows] - total * scale[rows]


VMEM = pl.BlockSpec(memory_space=pltpu.VMEM)
SMEM = pl.BlockSpec(memory_space=pltpu.SMEM)
ANY = pl.BlockSpec(memory_space=pl.ANY)


def call(body, outs, in_specs, args, scratch=(), micros=0.0, name=None):
    return pl.pallas_call(
        body,
        out_shape=[x if hasattr(x, "dtype") else jax.ShapeDtypeStruct(x, F32) for x in outs],
        in_specs=in_specs,
        out_specs=[VMEM] * len(outs),
        scratch_shapes=list(scratch),
        compiler_params=pltpu.CompilerParams(vmem_limit_bytes=24 * 1024 * 1024),
        cost_estimate=pl.CostEstimate(flops=int(micros * 1e9), bytes_accessed=1, transcendentals=0),
        name=name,
    )(*args)


def shards(object_field, probe, positions, residual, saved_wave):
    window = probe.shape[-1]
    half = window // 2
    count = positions.shape[0]
    size = notes_size(count)
    table = jnp.asarray(tables(window))
    barrier = lax.optimization_barrier

    def twice(*planes):
        return pltpu.VMEM((*planes, 2 * window + 8, window), F32)

    grads = pltpu.VMEM((2, count, window, window), F32)
    pos_scratch = [pltpu.SMEM(positions.shape, jnp.int32), pltpu.SemaphoreType.DMA]
    fields_shape = (count, 2, window, window)
    wide_shape = (2, window, 2 * window)
    square, strip = (2, half, window), (2, window, half)

    edge_first, edge_second = call(
        edges, [strip] * 2, [VMEM], (object_field,), micros=12.0, name="edges"
    )
    halo_first = swapped(edge_first, "gx", 0)
    halo_second = swapped(edge_second, "gx", 1)

    field, up2, down2, middle2, notes, marks = call(
        detect,
        [fields_shape]
        + [(2, half + size, 2 * window)] * 2
        + [wide_shape, (size, half), jax.ShapeDtypeStruct((2 * count, 8, window), jnp.int32)],
        [ANY] + [VMEM] * 3,
        (positions, residual, saved_wave, table),
        [twice(count, 2), grads] + pos_scratch,
        micros=12.0, name="detect",
    )
    from_up2 = swapped(up2, "gy", 0)
    from_down2 = swapped(down2, "gy", 1)

    fields, probes = call(
        roll_fields,
        [fields_shape] * 2,
        [ANY] + [VMEM] * 2,
        (positions, field, probe),
        [twice(count + 1, 2)] + pos_scratch,
        micros=0.1, name="roll",
    )
    rows_first, rows_second = call(
        relay,
        [(2, half, 2 * window)] * 2,
        [VMEM] * 3,
        (object_field, halo_first, halo_second),
        micros=12.0, name="widen",
    )
    from_rows_first = swapped(rows_first, "gy", 0)
    from_rows_second = swapped(rows_second, "gy", 1)

    from_up2, from_down2, fields, probes = barrier((from_up2, from_down2, fields, probes))
    first2, second2, centre2 = call(
        narrow,
        [(2, window + 3 * size, half)] * 2 + [fields_shape[1:]],
        [VMEM] * 4,
        (notes, middle2, from_up2, from_down2),
        micros=0.2, name="narrow2",
    )
    from_rows_first, from_rows_second, centre2 = barrier((from_rows_first, from_rows_second, centre2))
    got_first2 = swapped(first2, "gx", 0)
    got_second2 = swapped(second2, "gx", 1)

    outer_first, outer_second, inner_first, inner_second, middle1 = call(
        propagate,
        [square] * 4 + [wide_shape],
        [VMEM] * 9,
        (marks, fields, probes, object_field, halo_first, halo_second, from_rows_first, from_rows_second, table),
        [pltpu.VMEM(fields_shape, BF16)] * 2 + [grads],
        micros=0.1, name="propagate",
    )
    from_outer_first = swapped(outer_first, "gy", 0)
    from_outer_second = swapped(outer_second, "gy", 1)
    (total2_first,) = call(
        functools.partial(join, low=False), [strip], [VMEM] * 2, (centre2, got_first2), micros=1.0, name="join2"
    )
    middle1, total2_first = barrier((middle1, total2_first))
    first1, second1 = call(
        narrow_outer, [strip] * 2, [VMEM] * 3, (middle1, from_outer_first, from_outer_second), micros=0.2, name="narrow1"
    )
    got_first1 = swapped(first1, "gx", 0)
    got_second1 = swapped(second1, "gx", 1)
    from_inner_first = swapped(inner_first, "gy", 0)
    from_inner_second = swapped(inner_second, "gy", 1)

    from_inner_first, from_inner_second, got_first2, got_second2 = barrier(
        (from_inner_first, from_inner_second, got_first2, got_second2)
    )
    (scale,) = call(
        illuminate,
        [(window, window)],
        [SMEM] + [VMEM] * 5,
        (positions, probe, from_up2, from_down2, got_first2, got_second2),
        [twice(), pltpu.SMEM((8 * size, half), F32), pltpu.SemaphoreType.DMA((4,))],
        micros=12.0, name="illuminate",
    )
    (total2_second,) = call(
        functools.partial(join, low=True), [strip], [VMEM] * 2, (centre2, got_second2), micros=0.1, name="join3"
    )
    (new_object,) = call(
        update,
        [object_field.shape],
        [VMEM] * 9,
        (got_first1, got_second1, object_field, scale, total2_first, total2_second)
        + (middle1, from_inner_first, from_inner_second),
        micros=1.0, name="update",
    )
    return new_object


def solution(mesh):
    placed = (
        P(None, None, "gy", "gx"),
        P(),
        P("gy", "gx", None),
        P("gy", "gx", None, None, None),
        P("gy", "gx", None, None, None),
    )
    return jax.shard_map(
        shards, mesh=mesh, in_specs=placed, out_specs=P(None, None, "gy", "gx"), check_vma=False
    )
```

```python
import functools

import jax
import jax.numpy as jnp
import ml_dtypes
import numpy as np
from jax import lax
from jax.experimental import pallas as pl
from jax.experimental.pallas import tpu as pltpu
from jax.sharding import PartitionSpec as P

fresnel_rate = 200.0
ridge = 0.5
CHUNK = 32
F32 = jnp.float32
BF16 = jnp.bfloat16


def two_parts(table):
    high = table.astype(np.float32).astype(ml_dtypes.bfloat16)
    low = (table - high.astype(np.float64)).astype(ml_dtypes.bfloat16)
    return high, low


@functools.lru_cache(maxsize=None)
def tables(size):
    index = np.arange(size)
    inverse = np.exp(2j * np.pi * (np.outer(index, index) % size) / size) / np.sqrt(size)
    freq = ((index + size // 2) % size - size // 2) / size
    move = inverse @ np.diag(np.exp(1j * fresnel_rate * freq**2)) @ inverse.conj()
    out = []
    for matrix in (inverse, move):
        out.extend(two_parts(np.concatenate([matrix.real, matrix.imag], axis=1)))
    return np.stack(out)


def swap_pairs(count, first):
    pairs = []
    for low in range(first, count - 1, 2):
        pairs += [(low, low + 1), (low + 1, low)]
    return pairs


def swapped(value, axis, first):
    return lax.ppermute(value, axis, swap_pairs(lax.axis_size(axis), first))


def dot(a, b):
    return jnp.dot(a, b, preferred_element_type=F32)


def split(value):
    high = value.astype(BF16)
    return high, (value - high.astype(F32)).astype(BF16)


def place(waves, corners, out_first, out_second, out_middle, odd, window):
    half = window // 2

    def rows(base, lower, store):
        for start in range(0, half, CHUNK):
            at = pl.multiple_of(base + start, CHUNK)
            row = lax.broadcasted_iota(jnp.int32, (CHUNK, window), 0) + at
            col = lax.broadcasted_iota(jnp.int32, (CHUNK, window), 1)
            masks = []
            for r, c in corners:
                inside = (row < r) == (lower == 1)
                masks.append((inside & (col >= c), inside & (col < c)))
            for plane in range(len(waves)):
                left = right = None
                for number, (in_left, in_right) in enumerate(masks):
                    value = waves[plane][number, pl.ds(at, CHUNK), :]
                    a = jnp.where(in_left, value, 0.0)
                    b = jnp.where(in_right, value, 0.0)
                    left = a if left is None else left + a
                    right = b if right is None else right + b
                store(plane, start, left, right)

    def writer(ref, offset):
        def store(plane, start, left, right):
            at = slice(offset + start, offset + start + CHUNK)
            if isinstance(ref, tuple):
                ref[0][plane, at, :half] = left[:, :half]
                ref[0][plane, at, half:] = right[:, half:]
                ref[1][plane, at, :half] = left[:, half:]
                ref[1][plane, at, half:] = right[:, :half]
            else:
                ref[plane, at, :window] = left
                ref[plane, at, window:] = right

        return store

    rows((1 - odd) * half, 1 - odd, writer(out_first, 0))
    rows(odd * half, odd, writer(out_second, 0))
    rows(half, 0, writer(out_middle, 0))
    rows(0, 1, writer(out_middle, half))


def from_right(rows_re, rows_im, high, low, passes):
    window = high.shape[0]
    sums = []
    for rows in (rows_re, rows_im):
        total = dot(rows[0], high[...]) + dot(rows[0], low[...])
        if passes == 3:
            total += dot(rows[1], high[...])
        sums.append(total)
    one, two = sums
    return one[:, :window] - two[:, window:], one[:, window:] + two[:, :window]


def from_left(high, low, inner_hi, inner_lo):
    window = high.shape[0]
    sums = []
    for part in range(2):
        cols = slice(part * window, (part + 1) * window)
        sums.append(dot(high[:, cols], inner_hi) + dot(low[:, cols], inner_hi) + dot(high[:, cols], inner_lo))
    one, two = sums
    return one[:, :window] - two[:, window:], one[:, window:] + two[:, :window]


def rolled(twice, corner, store, window):
    r, c = corner
    rest = lax.rem(window - r, 8)
    back = lax.rem(CHUNK + 8 - rest, CHUNK + 8)
    for start in range(0, window, CHUNK):
        value = twice[pl.ds(pl.multiple_of(window - r - rest + start, 8), CHUNK + 8), :]
        store(start, pltpu.roll(pltpu.roll(value, back, 0)[:CHUNK], c, 1))


def twofold(twice, start, value, window):
    rows = value.shape[0]
    twice[start : start + rows] = value
    twice[window + start : window + start + rows] = value
    if start == 0:
        twice[2 * window : 2 * window + 8] = value[:8]


def corners_of(pos):
    return [(pos[number, 0, 0], pos[number, 0, 1]) for number in range(pos.shape[0])]


def fetched(pos_any, pos, sem):
    copy = pltpu.make_async_copy(pos_any, pos, sem)
    copy.start()
    return copy


def detect(
    pos_any, residual, wave, table, object_field,
    field, first, second, inner_first, inner_second, middle, notes, marks,
    twice, grads, pos, sem,
):
    window = residual.shape[-1]
    count = residual.shape[0]
    odd = lax.rem(lax.axis_index("gy"), 2)
    arrival = fetched(pos_any, pos, sem)
    table_hi, table_lo = table.at[0], table.at[1]
    for number in range(count):
        line = from_right((residual[number, 0, 0],), (residual[number, 0, 1],), table_hi, table_lo, 2)
        high, low = split(jnp.concatenate(line, axis=1))
        field_re, field_im = from_left(table_hi, table_lo, high, low)
        field[number, 0] = field_re
        field[number, 1] = field_im
        for start in range(0, window, CHUNK):
            rows = slice(start, start + CHUNK)
            wave_re, wave_im = wave[number, 0, 0, rows].astype(F32), wave[number, 0, 1, rows].astype(F32)
            value_re, value_im = field[number, 0, rows], field[number, 1, rows]
            twofold(twice.at[number, 0], start, wave_re * value_re + wave_im * value_im, window)
            twofold(twice.at[number, 1], start, wave_re * value_im - wave_im * value_re, window)
    arrival.wait()
    corners = corners_of(pos)
    for number, corner in enumerate(corners):
        for part in range(2):

            def store(start, value):
                grads[part, number, start : start + CHUNK] = value

            rolled(twice.at[number, part], corner, store, window)
            marks[2 * number + part] = jnp.full(marks.shape[1:], corner[part], jnp.int32)
    place([grads.at[0], grads.at[1]], corners, (first, inner_first), (second, inner_second), middle, odd, window)
    half = window // 2
    for ref, base in ((first, (1 - odd) * half), (second, odd * half)):
        ref[0, half:] = notes_of(pos, count, window)
        for part in range(2):
            ref[2 + part, :half] = object_field[1, part, pl.ds(pl.multiple_of(base, half), half), :]
    notes[...] = notes_of(pos, count, window // 2)


def roll_fields(pos_any, field, probe, field_out, probes, twice, pos, sem):
    window = probe.shape[-1]
    count = field.shape[0]
    arrival = fetched(pos_any, pos, sem)
    for part in range(2):
        for start in range(0, window, CHUNK):
            twofold(twice.at[count, part], start, probe[part, start : start + CHUNK], window)
            for number in range(count):
                twofold(twice.at[number, part], start, field[number, part, start : start + CHUNK], window)
    arrival.wait()
    for number, corner in enumerate(corners_of(pos)):
        for part in range(2):

            def to_field(start, value):
                field_out[number, part, start : start + CHUNK] = value

            rolled(twice.at[number, part], corner, to_field, window)

            def to_probes(start, value):
                probes[number, part, start : start + CHUNK] = value

            rolled(twice.at[count, part], corner, to_probes, window)


def notes_size(count):
    return -(-(1 + 2 * count) // 8) * 8


def notes_of(pos, count, width):
    size = notes_size(count)
    row = lax.broadcasted_iota(jnp.int32, (size, width), 0)
    notes = jnp.where(row == 0, 1, 0)
    for number in range(count):
        for part in range(2):
            notes = jnp.where(row == 1 + 2 * number + part, pos[number, 0, part], notes)
    return notes.astype(F32)


def sides(odd, one, two):
    return jnp.where(odd == 1, one, two), jnp.where(odd == 1, two, one)


def edges(object_field, first, second):
    half = object_field.shape[-1] // 2
    odd_x = lax.rem(lax.axis_index("gx"), 2)
    for ref, odd in ((first, 1 - odd_x), (second, odd_x)):
        ref[...] = object_field[1, :, :, pl.ds(pl.multiple_of(odd * half, half), half)]


def relay(from_first, from_second, first, second):
    half = from_first.shape[-1]
    odd_x = lax.rem(lax.axis_index("gx"), 2)
    odd_y = lax.rem(lax.axis_index("gy"), 2)
    at_first = pl.ds(pl.multiple_of((1 - odd_x) * half, half), half)
    at_second = pl.ds(pl.multiple_of(odd_x * half, half), half)
    for ref, base in ((first, (1 - odd_y) * half), (second, odd_y * half)):
        rows = pl.ds(pl.multiple_of(base, half), half)
        for plane in range(ref.shape[0]):
            ref[plane, :, at_first] = from_first[plane, rows]
            ref[plane, :, at_second] = from_second[plane, rows]


def propagate(
    marks, field, probes, object_field, halo_first, halo_second,
    own_second, own_first, corner_second, corner_first, table, inner2_first, inner2_second,
    outer_first, outer_second, inner_first, inner_second, middle,
    chi_hi, chi_lo, grads,
):
    window = field.shape[-1]
    half = window // 2
    count = field.shape[0]
    odd_x = lax.rem(lax.axis_index("gx"), 2)
    odd = lax.rem(lax.axis_index("gy"), 2)
    corners = [(marks[2 * number, :1], marks[2 * number + 1, :1]) for number in range(count)]
    table_hi, table_lo = table.at[2], table.at[3]
    inner_first[2:] = inner2_first[...]
    inner_second[2:] = inner2_second[...]

    def wide(part, rows):
        left, right = sides(odd_x, halo_first[part, rows], halo_second[part, rows])
        return jnp.concatenate([left, object_field[1, part, rows], right], axis=1)

    def beyond(part, rows, below):
        own = sides(odd, own_first[2 + part, rows], own_second[2 + part, rows])[below]
        corner = sides(odd, corner_first[part, rows], corner_second[part, rows])[below]
        return jnp.concatenate([corner[:, :half], own, corner[:, half:]], axis=1)

    for start in range(0, window, CHUNK):
        rows = slice(start, start + CHUNK)
        row = lax.broadcasted_iota(jnp.int32, (CHUNK, window), 0) + start
        col = lax.broadcasted_iota(jnp.int32, (CHUNK, window), 1)
        upper, lower = [], []
        for part in range(2):
            if start < half:
                upper.append(beyond(part, rows, 0))
                lower.append(wide(part, slice(half + start, half + start + CHUNK)))
            else:
                shifted = slice(start - half, start - half + CHUNK)
                upper.append(wide(part, shifted))
                lower.append(beyond(part, shifted, 1))
        for number, (r, c) in enumerate(corners):
            low_row, low_col = row < r, col < c
            patch = []
            for part in range(2):
                above = jnp.where(low_col, upper[part][:, window:], upper[part][:, :window])
                below = jnp.where(low_col, lower[part][:, window:], lower[part][:, :window])
                patch.append(jnp.where(low_row, below, above))
            field_re, field_im = field[number, 0, rows], field[number, 1, rows]
            high, low = split(patch[0] * field_re + patch[1] * field_im)
            chi_hi[number, 0, rows] = high
            chi_lo[number, 0, rows] = low
            high, low = split(patch[0] * field_im - patch[1] * field_re)
            chi_hi[number, 1, rows] = high
            chi_lo[number, 1, rows] = low

    for number in range(count):
        line = from_right(
            (chi_hi[number, 0], chi_lo[number, 0]), (chi_hi[number, 1], chi_lo[number, 1]), table_hi, table_lo, 3
        )
        high, low = split(jnp.concatenate(line, axis=1))
        back_re, back_im = from_left(table_hi, table_lo, high, low)
        probe_re, probe_im = probes[number, 0], probes[number, 1]
        grads[0, number] = probe_re * back_re + probe_im * back_im
        grads[1, number] = probe_re * back_im - probe_im * back_re
    place(
        [grads.at[0], grads.at[1]], corners, (outer_first, inner_first), (outer_second, inner_second), middle, odd, window
    )


def illuminate(pos, probe, up, down, first, second, scale, twice, notes, sems):
    window = probe.shape[-1]
    half = window // 2
    count = pos.shape[0]
    size = notes_size(count)
    odd_x = lax.rem(lax.axis_index("gx"), 2)
    odd_y = lax.rem(lax.axis_index("gy"), 2)
    copies, at = [], 0
    for ref, start, rows in ((up, half, size), (down, half, size), (first, window, 3 * size), (second, window, 3 * size)):
        source = ref.at[0, pl.ds(start, rows), pl.ds(0, half)]
        copies.append(pltpu.make_async_copy(source, notes.at[pl.ds(at, rows), :], sems.at[len(copies)]))
        copies[-1].start()
        at += rows
    for start in range(0, window, CHUNK):
        rows = slice(start, start + CHUNK)
        twofold(twice, start, probe[0, rows] * probe[0, rows] + probe[1, rows] * probe[1, rows], window)
    for copy in copies:
        copy.wait()

    shifts = []
    for down in (-1, 0, 1):
        for along in (-1, 0, 1):
            if along == 0:
                base = (odd_y if down > 0 else 1 - odd_y) * size
            else:
                base = (2 + 3 * (odd_x if along > 0 else 1 - odd_x) + 1 + down) * size
            for number in range(count):
                if down == 0 and along == 0:
                    valid, r, c = 1, pos[number, 0, 0], pos[number, 0, 1]
                else:
                    valid, r, c = (
                        notes[base + row, 0].astype(jnp.int32) for row in (0, 1 + 2 * number, 2 + 2 * number)
                    )
                top = r - half + window * down
                left = c - half + window * along
                top = jnp.where(valid == 1, top, window)
                shifts.append((top, left, r, c))

    def rows_at(index, carry):
        start = index * CHUNK
        row = lax.broadcasted_iota(jnp.int32, (CHUNK, window), 0) + start
        col = lax.broadcasted_iota(jnp.int32, (CHUNK, window), 1)
        total = jnp.zeros((CHUNK, window), F32)
        for top, left, r, c in shifts:
            turn = lax.rem(2 * window - half - r, window)
            rest = lax.rem(turn, 8)
            value = twice[pl.ds(pl.multiple_of(turn - rest + start, 8), CHUNK + 8), :]
            value = pltpu.roll(value, lax.rem(CHUNK + 8 - rest, CHUNK + 8), 0)[:CHUNK]
            value = pltpu.roll(value, lax.rem(c + half, window), 1)
            inside = (row >= top) & (row < top + window) & (col >= left) & (col < left + window)
            total += jnp.where(inside, value, 0.0)
        scale[pl.ds(pl.multiple_of(start, CHUNK), CHUNK), :] = 1.0 / (total + ridge)
        return carry

    lax.fori_loop(0, window // CHUNK, rows_at, 0)


def narrow_noted(notes, middle, from_second, from_first, first, second):
    half = first.shape[-1]
    window = 2 * half
    odd_y = lax.rem(lax.axis_index("gy"), 2)
    columns = pl.ds(0, window)
    narrow_outer(
        middle, from_second.at[:2, :half], from_first.at[:2, :half], first.at[:, columns], second.at[:, columns]
    )
    size = notes.shape[0]
    above, below = sides(odd_y, from_first[0, half:, :half], from_second[0, half:, :half])
    for ref in (first, second):
        ref[0, window : window + size] = above
        ref[0, window + size : window + 2 * size] = notes[...]
        ref[0, window + 2 * size :] = below


def narrow_outer(middle, from_second, from_first, first, second):
    half = first.shape[-1]
    odd_x = lax.rem(lax.axis_index("gx"), 2)
    odd_y = lax.rem(lax.axis_index("gy"), 2)
    for plane in range(middle.shape[0]):
        for received, base in ((from_first, (1 - odd_y) * half), (from_second, odd_y * half)):
            at = pl.ds(pl.multiple_of(base, half), half)
            left = middle[plane, at, :half] + received[plane, :, :half]
            right = middle[plane, at, 3 * half :] + received[plane, :, half:]
            second[plane, at, :], first[plane, at, :] = sides(odd_x, right, left)


def join(middle, received, out, low):
    window = middle.shape[1]
    half = window // 2
    odd_x = lax.rem(lax.axis_index("gx"), 2)
    base = (odd_x if low else 1 - odd_x) * half
    at = pl.ds(pl.multiple_of(half + base, half), half)
    out[...] = middle[:, :, at] + received[:, :window]


def written(value, out, number, sem):
    copy = pltpu.make_async_copy(value, out.at[number], sem)
    copy.start()
    return copy


def update_second(
    object_field, scale, total2_first, total2_second, inner_second, inner_first, out, value, sem
):
    half = scale.shape[-1] // 2
    odd_x = lax.rem(lax.axis_index("gx"), 2)
    odd_y = lax.rem(lax.axis_index("gy"), 2)
    for part in range(2):
        for received, base in ((inner_first, (1 - odd_y) * half), (inner_second, odd_y * half)):
            rows = pl.ds(pl.multiple_of(base, half), half)
            outer = jnp.concatenate(sides(odd_x, total2_first[part, rows], total2_second[part, rows]), axis=1)
            value[part, rows] = object_field[1, part, rows] - (outer + received[2 + part]) * scale[rows]
    written(value, out, 1, sem).wait()


def update_first(
    begun, first1, second1, object_field, scale, middle1, inner_second, inner_first, out, value, sems
):
    del begun
    window = scale.shape[-1]
    half = window // 2
    odd_x = lax.rem(lax.axis_index("gx"), 2)
    odd_y = lax.rem(lax.axis_index("gy"), 2)
    copies = []
    for part in range(2):
        for received, base in ((inner_first, (1 - odd_y) * half), (inner_second, odd_y * half)):
            rows = pl.ds(pl.multiple_of(base, half), half)
            outer = jnp.concatenate(sides(odd_x, first1[part, rows], second1[part, rows]), axis=1)
            total = middle1[part, rows, half : 3 * half] + received[part] + outer
            value[part, rows] = object_field[0, part, rows] - total * scale[rows]
        copies.append(written(value.at[part], out.at[0], part, sems.at[part]))
    for copy in copies:
        copy.wait()


VMEM = pl.BlockSpec(memory_space=pltpu.VMEM)
SMEM = pl.BlockSpec(memory_space=pltpu.SMEM)
ANY = pl.BlockSpec(memory_space=pl.ANY)


def call(body, outs, in_specs, args, scratch=(), out_specs=None, aliases=None, micros=0.0, name=None):
    return pl.pallas_call(
        body,
        out_shape=[x if hasattr(x, "dtype") else jax.ShapeDtypeStruct(x, F32) for x in outs],
        in_specs=in_specs,
        out_specs=out_specs or [VMEM] * len(outs),
        input_output_aliases=aliases or {},
        scratch_shapes=list(scratch),
        compiler_params=pltpu.CompilerParams(vmem_limit_bytes=24 * 1024 * 1024),
        cost_estimate=pl.CostEstimate(flops=int(micros * 1e9), bytes_accessed=1, transcendentals=0),
        name=name,
    )(*args)


def shards(object_field, probe, positions, residual, saved_wave):
    window = probe.shape[-1]
    half = window // 2
    count = positions.shape[0]
    size = notes_size(count)
    table = jnp.asarray(tables(window))
    barrier = lax.optimization_barrier

    def twice(*planes):
        return pltpu.VMEM((*planes, 2 * window + 8, window), F32)

    grads = pltpu.VMEM((2, count, window, window), F32)
    pos_scratch = [pltpu.SMEM(positions.shape, jnp.int32), pltpu.SemaphoreType.DMA]
    fields_shape = (count, 2, window, window)
    wide_shape = (2, window, 2 * window)
    square, strip = (2, half, window), (2, window, half)

    edge_first, edge_second = call(
        edges, [strip] * 2, [VMEM], (object_field,), micros=12.0, name="edges"
    )
    halo_first = swapped(edge_first, "gx", 0)
    halo_second = swapped(edge_second, "gx", 1)

    field, up2, down2, inner2_first, inner2_second, middle2, notes, marks = call(
        detect,
        [fields_shape]
        + [(4, half + size, window)] * 2
        + [square, square, wide_shape, (size, half), jax.ShapeDtypeStruct((2 * count, 8, window), jnp.int32)],
        [ANY] + [VMEM] * 4,
        (positions, residual, saved_wave, table, object_field),
        [twice(count, 2), grads] + pos_scratch,
        micros=12.0, name="detect",
    )
    from_down2 = swapped(down2, "gy", 1)
    from_up2 = swapped(up2, "gy", 0)

    fields, probes = call(
        roll_fields,
        [fields_shape] * 2,
        [ANY] + [VMEM] * 2,
        (positions, field, probe),
        [twice(count + 1, 2)] + pos_scratch,
        micros=0.1, name="roll",
    )
    rows_first, rows_second = call(
        relay,
        [square] * 2,
        [VMEM] * 2,
        (halo_first, halo_second),
        micros=12.0, name="widen",
    )
    from_rows_second = swapped(rows_second, "gy", 1)
    from_rows_first = swapped(rows_first, "gy", 0)

    from_down2, from_up2, fields, probes = barrier((from_down2, from_up2, fields, probes))
    first2, second2 = call(
        narrow_noted,
        [(2, window + 3 * size, half)] * 2,
        [VMEM] * 4,
        (notes, middle2, from_down2, from_up2),
        micros=0.2, name="narrow2",
    )
    from_rows_second, from_rows_first, marks, _ = barrier((from_rows_second, from_rows_first, marks, first2))
    got_first2 = swapped(first2, "gx", 0)
    got_second2 = swapped(second2, "gx", 1)

    outer_first, outer_second, inner_first, inner_second, middle1 = call(
        propagate,
        [square] * 2 + [(4, half, window)] * 2 + [wide_shape],
        [VMEM] * 13,
        (marks, fields, probes, object_field, halo_first, halo_second, from_down2, from_up2)
        + (from_rows_second, from_rows_first, table, inner2_first, inner2_second),
        [pltpu.VMEM(fields_shape, BF16)] * 2 + [grads],
        micros=0.1, name="propagate",
    )
    from_outer_second = swapped(outer_second, "gy", 1)
    from_outer_first = swapped(outer_first, "gy", 0)
    (total2_second,) = call(
        functools.partial(join, low=True), [strip], [VMEM] * 2, (middle2, got_second2), micros=1.0, name="join3"
    )
    middle1, total2_second = barrier((middle1, total2_second))
    first1, second1 = call(
        narrow_outer, [strip] * 2, [VMEM] * 3, (middle1, from_outer_second, from_outer_first), micros=0.2, name="narrow1"
    )
    got_first1 = swapped(first1, "gx", 0)
    got_second1 = swapped(second1, "gx", 1)
    from_inner_first = swapped(inner_first, "gy", 0)
    from_inner_second = swapped(inner_second, "gy", 1)

    (scale,) = call(
        illuminate,
        [(window, window)],
        [SMEM] + [VMEM] * 5,
        (positions, probe, from_up2, from_down2, got_first2, got_second2),
        [twice(), pltpu.SMEM((8 * size, half), F32), pltpu.SemaphoreType.DMA((4,))],
        micros=12.0, name="illuminate",
    )
    (total2_first,) = call(
        functools.partial(join, low=False), [strip], [VMEM] * 2, (middle2, got_first2), micros=0.5, name="join2"
    )
    value = pltpu.VMEM(fields_shape[1:], F32)
    (begun,) = call(
        update_second,
        [object_field.shape],
        [VMEM] * 6,
        (object_field, scale, total2_first, total2_second, from_inner_second, from_inner_first),
        [value, pltpu.SemaphoreType.DMA],
        out_specs=[ANY], micros=0.1, name="update2",
    )
    (new_object,) = call(
        update_first,
        [object_field.shape],
        [ANY] + [VMEM] * 7,
        (begun, got_first1, got_second1, object_field, scale, middle1, from_inner_second, from_inner_first),
        [value, pltpu.SemaphoreType.DMA((2,))],
        out_specs=[ANY], aliases={0: 0}, micros=1.0, name="update",
    )
    return new_object


def solution(mesh):
    placed = (
        P(None, None, "gy", "gx"),
        P(),
        P("gy", "gx", None),
        P("gy", "gx", None, None, None),
        P("gy", "gx", None, None, None),
    )
    return jax.shard_map(
        shards, mesh=mesh, in_specs=placed, out_specs=P(None, None, "gy", "gx"), check_vma=False
    )
```

```python
import functools

import jax
import jax.numpy as jnp
import ml_dtypes
import numpy as np
from jax import lax
from jax.experimental import pallas as pl
from jax.experimental.pallas import tpu as pltpu
from jax.sharding import PartitionSpec as P

fresnel_rate = 200.0
ridge = 0.5
CHUNK = 32
F32 = jnp.float32
BF16 = jnp.bfloat16


def two_parts(table):
    high = table.astype(np.float32).astype(ml_dtypes.bfloat16)
    low = (table - high.astype(np.float64)).astype(ml_dtypes.bfloat16)
    return high, low


@functools.lru_cache(maxsize=None)
def tables(size):
    index = np.arange(size)
    inverse = np.exp(2j * np.pi * (np.outer(index, index) % size) / size) / np.sqrt(size)
    freq = ((index + size // 2) % size - size // 2) / size
    move = inverse @ np.diag(np.exp(1j * fresnel_rate * freq**2)) @ inverse.conj()
    out = []
    for matrix in (inverse, move):
        out.extend(two_parts(np.concatenate([matrix.real, matrix.imag], axis=1)))
    return np.stack(out)


def swap_pairs(count, first):
    pairs = []
    for low in range(first, count - 1, 2):
        pairs += [(low, low + 1), (low + 1, low)]
    return pairs


def swapped(value, axis, first):
    return lax.ppermute(value, axis, swap_pairs(lax.axis_size(axis), first))


def around(value, axis):
    count = lax.axis_size(axis)
    if count % 2 or count < 4:
        return swapped(value, axis, 1)
    out, back = [], []
    for low in range(1, count - 1, 2):
        out += [(low, low + 2), (low + 1, low - 1)]
        back += [(low + 2, low + 1), (low - 1, low)]
    return lax.ppermute(lax.ppermute(value, axis, out), axis, back)


def dot(a, b):
    return jnp.dot(a, b, preferred_element_type=F32)


def split(value):
    high = value.astype(BF16)
    return high, (value - high.astype(F32)).astype(BF16)


def place(waves, corners, out_first, out_second, out_middle, odd, window):
    half = window // 2

    def rows(base, lower, store):
        for start in range(0, half, CHUNK):
            at = pl.multiple_of(base + start, CHUNK)
            row = lax.broadcasted_iota(jnp.int32, (CHUNK, window), 0) + at
            col = lax.broadcasted_iota(jnp.int32, (CHUNK, window), 1)
            masks = []
            for r, c in corners:
                inside = (row < r) == (lower == 1)
                masks.append((inside & (col >= c), inside & (col < c)))
            for plane in range(len(waves)):
                left = right = None
                for number, (in_left, in_right) in enumerate(masks):
                    value = waves[plane][number, pl.ds(at, CHUNK), :]
                    a = jnp.where(in_left, value, 0.0)
                    b = jnp.where(in_right, value, 0.0)
                    left = a if left is None else left + a
                    right = b if right is None else right + b
                store(plane, start, left, right)

    def writer(ref, offset):
        def store(plane, start, left, right):
            at = slice(offset + start, offset + start + CHUNK)
            if isinstance(ref, tuple):
                ref[0][plane, at, :half] = left[:, :half]
                ref[0][plane, at, half:] = right[:, half:]
                ref[1][plane, at, :half] = left[:, half:]
                ref[1][plane, at, half:] = right[:, :half]
            else:
                ref[plane, at, :window] = left
                ref[plane, at, window:] = right

        return store

    rows((1 - odd) * half, 1 - odd, writer(out_first, 0))
    rows(odd * half, odd, writer(out_second, 0))
    rows(half, 0, writer(out_middle, 0))
    rows(0, 1, writer(out_middle, half))


def from_right(rows_re, rows_im, high, low, passes):
    window = high.shape[0]
    sums = []
    for rows in (rows_re, rows_im):
        total = dot(rows[0], high[...]) + dot(rows[0], low[...])
        if passes == 3:
            total += dot(rows[1], high[...])
        sums.append(total)
    one, two = sums
    return one[:, :window] - two[:, window:], one[:, window:] + two[:, :window]


def from_left(high, low, inner_hi, inner_lo):
    window = high.shape[0]
    sums = []
    for part in range(2):
        cols = slice(part * window, (part + 1) * window)
        sums.append(dot(high[:, cols], inner_hi) + dot(low[:, cols], inner_hi) + dot(high[:, cols], inner_lo))
    one, two = sums
    return one[:, :window] - two[:, window:], one[:, window:] + two[:, :window]


def rolled(twice, corner, store, window):
    r, c = corner
    rest = lax.rem(window - r, 8)
    back = lax.rem(CHUNK + 8 - rest, CHUNK + 8)
    for start in range(0, window, CHUNK):
        value = twice[pl.ds(pl.multiple_of(window - r - rest + start, 8), CHUNK + 8), :]
        store(start, pltpu.roll(pltpu.roll(value, back, 0)[:CHUNK], c, 1))


def twofold(twice, start, value, window):
    rows = value.shape[0]
    twice[start : start + rows] = value
    twice[window + start : window + start + rows] = value
    if start == 0:
        twice[2 * window : 2 * window + 8] = value[:8]


def corners_of(pos):
    return [(pos[number, 0, 0], pos[number, 0, 1]) for number in range(pos.shape[0])]


def fetched(pos_any, pos, sem):
    copy = pltpu.make_async_copy(pos_any, pos, sem)
    copy.start()
    return copy


def detect(
    pos_any, residual, wave, table, object_field,
    field, first, second, inner_first, inner_second, middle, notes, marks,
    twice, grads, pos, sem,
):
    window = residual.shape[-1]
    count = residual.shape[0]
    odd = lax.rem(lax.axis_index("gy"), 2)
    arrival = fetched(pos_any, pos, sem)
    table_hi, table_lo = table.at[0], table.at[1]
    for number in range(count):
        line = from_right((residual[number, 0, 0],), (residual[number, 0, 1],), table_hi, table_lo, 2)
        high, low = split(jnp.concatenate(line, axis=1))
        field_re, field_im = from_left(table_hi, table_lo, high, low)
        field[number, 0] = field_re
        field[number, 1] = field_im
        for start in range(0, window, CHUNK):
            rows = slice(start, start + CHUNK)
            wave_re, wave_im = wave[number, 0, 0, rows].astype(F32), wave[number, 0, 1, rows].astype(F32)
            value_re, value_im = field[number, 0, rows], field[number, 1, rows]
            twofold(twice.at[number, 0], start, wave_re * value_re + wave_im * value_im, window)
            twofold(twice.at[number, 1], start, wave_re * value_im - wave_im * value_re, window)
    arrival.wait()
    corners = corners_of(pos)
    for number, corner in enumerate(corners):
        for part in range(2):

            def store(start, value):
                grads[part, number, start : start + CHUNK] = value

            rolled(twice.at[number, part], corner, store, window)
            marks[2 * number + part] = jnp.full(marks.shape[1:], corner[part], jnp.int32)
    place([grads.at[0], grads.at[1]], corners, (first, inner_first), (second, inner_second), middle, odd, window)
    half = window // 2
    for ref, base in ((first, (1 - odd) * half), (second, odd * half)):
        ref[0, half:] = notes_of(pos, count, window)
        for part in range(2):
            ref[2 + part, :half] = object_field[1, part, pl.ds(pl.multiple_of(base, half), half), :]
    notes[...] = notes_of(pos, count, window // 2)


def roll_fields(pos_any, field, probe, field_out, probes, twice, pos, sem):
    window = probe.shape[-1]
    count = field.shape[0]
    arrival = fetched(pos_any, pos, sem)
    for part in range(2):
        for start in range(0, window, CHUNK):
            twofold(twice.at[count, part], start, probe[part, start : start + CHUNK], window)
            for number in range(count):
                twofold(twice.at[number, part], start, field[number, part, start : start + CHUNK], window)
    arrival.wait()
    for number, corner in enumerate(corners_of(pos)):
        for part in range(2):

            def to_field(start, value):
                field_out[number, part, start : start + CHUNK] = value

            rolled(twice.at[number, part], corner, to_field, window)

            def to_probes(start, value):
                probes[number, part, start : start + CHUNK] = value

            rolled(twice.at[count, part], corner, to_probes, window)


def notes_size(count):
    return -(-(1 + 2 * count) // 8) * 8


def notes_of(pos, count, width):
    size = notes_size(count)
    row = lax.broadcasted_iota(jnp.int32, (size, width), 0)
    notes = jnp.where(row == 0, 1, 0)
    for number in range(count):
        for part in range(2):
            notes = jnp.where(row == 1 + 2 * number + part, pos[number, 0, part], notes)
    return notes.astype(F32)


def sides(odd, one, two):
    return jnp.where(odd == 1, one, two), jnp.where(odd == 1, two, one)


def edges(object_field, first, second):
    half = object_field.shape[-1] // 2
    odd_x = lax.rem(lax.axis_index("gx"), 2)
    for ref, odd in ((first, 1 - odd_x), (second, odd_x)):
        ref[...] = object_field[1, :, :, pl.ds(pl.multiple_of(odd * half, half), half)]


def relay(from_first, from_second, first, second):
    half = from_first.shape[-1]
    odd_x = lax.rem(lax.axis_index("gx"), 2)
    odd_y = lax.rem(lax.axis_index("gy"), 2)
    at_first = pl.ds(pl.multiple_of((1 - odd_x) * half, half), half)
    at_second = pl.ds(pl.multiple_of(odd_x * half, half), half)
    for ref, base in ((first, (1 - odd_y) * half), (second, odd_y * half)):
        rows = pl.ds(pl.multiple_of(base, half), half)
        for plane in range(ref.shape[0]):
            ref[plane, :, at_first] = from_first[plane, rows]
            ref[plane, :, at_second] = from_second[plane, rows]


def propagate(
    marks, field, probes, object_field, halo_first, halo_second,
    own_second, own_first, corner_second, corner_first, table, inner2_first, inner2_second,
    outer_first, outer_second, inner_first, inner_second, middle,
    chi_hi, chi_lo, grads,
):
    window = field.shape[-1]
    half = window // 2
    count = field.shape[0]
    odd_x = lax.rem(lax.axis_index("gx"), 2)
    odd = lax.rem(lax.axis_index("gy"), 2)
    corners = [(marks[2 * number, :1], marks[2 * number + 1, :1]) for number in range(count)]
    table_hi, table_lo = table.at[2], table.at[3]
    inner_first[2:] = inner2_first[...]
    inner_second[2:] = inner2_second[...]

    def wide(part, rows):
        left, right = sides(odd_x, halo_first[part, rows], halo_second[part, rows])
        return jnp.concatenate([left, object_field[1, part, rows], right], axis=1)

    def beyond(part, rows, below):
        own = sides(odd, own_first[2 + part, rows], own_second[2 + part, rows])[below]
        corner = sides(odd, corner_first[part, rows], corner_second[part, rows])[below]
        return jnp.concatenate([corner[:, :half], own, corner[:, half:]], axis=1)

    for start in range(0, window, CHUNK):
        rows = slice(start, start + CHUNK)
        row = lax.broadcasted_iota(jnp.int32, (CHUNK, window), 0) + start
        col = lax.broadcasted_iota(jnp.int32, (CHUNK, window), 1)
        upper, lower = [], []
        for part in range(2):
            if start < half:
                upper.append(beyond(part, rows, 0))
                lower.append(wide(part, slice(half + start, half + start + CHUNK)))
            else:
                shifted = slice(start - half, start - half + CHUNK)
                upper.append(wide(part, shifted))
                lower.append(beyond(part, shifted, 1))
        for number, (r, c) in enumerate(corners):
            low_row, low_col = row < r, col < c
            patch = []
            for part in range(2):
                above = jnp.where(low_col, upper[part][:, window:], upper[part][:, :window])
                below = jnp.where(low_col, lower[part][:, window:], lower[part][:, :window])
                patch.append(jnp.where(low_row, below, above))
            field_re, field_im = field[number, 0, rows], field[number, 1, rows]
            high, low = split(patch[0] * field_re + patch[1] * field_im)
            chi_hi[number, 0, rows] = high
            chi_lo[number, 0, rows] = low
            high, low = split(patch[0] * field_im - patch[1] * field_re)
            chi_hi[number, 1, rows] = high
            chi_lo[number, 1, rows] = low

    for number in range(count):
        line = from_right(
            (chi_hi[number, 0], chi_lo[number, 0]), (chi_hi[number, 1], chi_lo[number, 1]), table_hi, table_lo, 3
        )
        high, low = split(jnp.concatenate(line, axis=1))
        back_re, back_im = from_left(table_hi, table_lo, high, low)
        probe_re, probe_im = probes[number, 0], probes[number, 1]
        grads[0, number] = probe_re * back_re + probe_im * back_im
        grads[1, number] = probe_re * back_im - probe_im * back_re
    place(
        [grads.at[0], grads.at[1]], corners, (outer_first, inner_first), (outer_second, inner_second), middle, odd, window
    )


def illuminate(pos, probe, up, down, first, second, scale, twice, notes, sems):
    window = probe.shape[-1]
    half = window // 2
    count = pos.shape[0]
    size = notes_size(count)
    odd_x = lax.rem(lax.axis_index("gx"), 2)
    odd_y = lax.rem(lax.axis_index("gy"), 2)
    copies, at = [], 0
    for ref, start, rows in ((up, half, size), (down, half, size), (first, window, 3 * size), (second, window, 3 * size)):
        source = ref.at[0, pl.ds(start, rows), pl.ds(0, half)]
        copies.append(pltpu.make_async_copy(source, notes.at[pl.ds(at, rows), :], sems.at[len(copies)]))
        copies[-1].start()
        at += rows
    for start in range(0, window, CHUNK):
        rows = slice(start, start + CHUNK)
        twofold(twice, start, probe[0, rows] * probe[0, rows] + probe[1, rows] * probe[1, rows], window)
    for copy in copies:
        copy.wait()

    upper, lower = [], []
    for down in (-1, 0, 1):
        for along in (-1, 0, 1):
            if along == 0:
                base = (odd_y if down > 0 else 1 - odd_y) * size
            else:
                base = (2 + 3 * (odd_x if along > 0 else 1 - odd_x) + 1 + down) * size
            for number in range(count):
                if down == 0 and along == 0:
                    valid, r, c = 1, pos[number, 0, 0], pos[number, 0, 1]
                else:
                    valid, r, c = (
                        notes[base + row, 0].astype(jnp.int32) for row in (0, 1 + 2 * number, 2 + 2 * number)
                    )
                top = r - half + window * down
                left = c - half + window * along
                top = jnp.where(valid == 1, top, window)
                for reached, half_at in ((upper, -1), (lower, 1)):
                    if down in (0, half_at):
                        reached.append((top, left, r, c))

    def rows_at(index, carry, shifts):
        start = index * CHUNK
        row = lax.broadcasted_iota(jnp.int32, (CHUNK, window), 0) + start
        col = lax.broadcasted_iota(jnp.int32, (CHUNK, window), 1)
        total = jnp.zeros((CHUNK, window), F32)
        for top, left, r, c in shifts:
            turn = lax.rem(2 * window - half - r, window)
            rest = lax.rem(turn, 8)
            value = twice[pl.ds(pl.multiple_of(turn - rest + start, 8), CHUNK + 8), :]
            value = pltpu.roll(value, lax.rem(CHUNK + 8 - rest, CHUNK + 8), 0)[:CHUNK]
            value = pltpu.roll(value, lax.rem(c + half, window), 1)
            inside = (row >= top) & (row < top + window) & (col >= left) & (col < left + window)
            total += jnp.where(inside, value, 0.0)
        scale[pl.ds(pl.multiple_of(start, CHUNK), CHUNK), :] = 1.0 / (total + ridge)
        return carry

    lax.fori_loop(0, half // CHUNK, functools.partial(rows_at, shifts=upper), 0)
    lax.fori_loop(half // CHUNK, window // CHUNK, functools.partial(rows_at, shifts=lower), 0)


def narrow_noted(notes, middle, from_second, from_first, first, second):
    half = first.shape[-1]
    window = 2 * half
    odd_y = lax.rem(lax.axis_index("gy"), 2)
    columns = pl.ds(0, window)
    narrow_outer(
        middle, from_second.at[:2, :half], from_first.at[:2, :half], first.at[:, columns], second.at[:, columns]
    )
    size = notes.shape[0]
    above, below = sides(odd_y, from_first[0, half:, :half], from_second[0, half:, :half])
    for ref in (first, second):
        ref[0, window : window + size] = above
        ref[0, window + size : window + 2 * size] = notes[...]
        ref[0, window + 2 * size :] = below


def narrow_parts(middle, from_second, from_first, first, second_re, second_im, second):
    narrow_outer(middle, from_second, from_first, first, second)
    second_re[0] = second[0]
    second_im[0] = second[1]


def narrow_outer(middle, from_second, from_first, first, second):
    half = first.shape[-1]
    odd_x = lax.rem(lax.axis_index("gx"), 2)
    odd_y = lax.rem(lax.axis_index("gy"), 2)
    for plane in range(middle.shape[0]):
        for received, base in ((from_first, (1 - odd_y) * half), (from_second, odd_y * half)):
            at = pl.ds(pl.multiple_of(base, half), half)
            left = middle[plane, at, :half] + received[plane, :, :half]
            right = middle[plane, at, 3 * half :] + received[plane, :, half:]
            second[plane, at, :], first[plane, at, :] = sides(odd_x, right, left)


def join(middle, received, out, low):
    window = middle.shape[1]
    half = window // 2
    odd_x = lax.rem(lax.axis_index("gx"), 2)
    base = (odd_x if low else 1 - odd_x) * half
    at = pl.ds(pl.multiple_of(half + base, half), half)
    out[...] = middle[:, :, at] + received[:, :window]


def written(value, out, number, sem):
    copy = pltpu.make_async_copy(value, out.at[number], sem)
    copy.start()
    return copy


def update_second(
    object_field, scale, total2_first, total2_second, inner_second, inner_first, out, value, sem
):
    half = scale.shape[-1] // 2
    odd_x = lax.rem(lax.axis_index("gx"), 2)
    odd_y = lax.rem(lax.axis_index("gy"), 2)
    for part in range(2):
        for received, base in ((inner_first, (1 - odd_y) * half), (inner_second, odd_y * half)):
            rows = pl.ds(pl.multiple_of(base, half), half)
            outer = jnp.concatenate(sides(odd_x, total2_first[part, rows], total2_second[part, rows]), axis=1)
            value[part, rows] = object_field[1, part, rows] - (outer + received[2 + part]) * scale[rows]
    written(value, out, 1, sem).wait()


def update_first(
    begun, first1, second1_re, second1_im, object_field, scale, middle1, inner_second, inner_first, out, value, sems
):
    del begun
    window = scale.shape[-1]
    half = window // 2
    odd_x = lax.rem(lax.axis_index("gx"), 2)
    odd_y = lax.rem(lax.axis_index("gy"), 2)
    copies = []
    for part in range(2):
        for received, base in ((inner_first, (1 - odd_y) * half), (inner_second, odd_y * half)):
            rows = pl.ds(pl.multiple_of(base, half), half)
            outer = jnp.concatenate(sides(odd_x, first1[part, rows], (second1_re, second1_im)[part][0, rows]), axis=1)
            total = middle1[part, rows, half : 3 * half] + received[part] + outer
            value[part, rows] = object_field[0, part, rows] - total * scale[rows]
        copies.append(written(value.at[part], out.at[0], part, sems.at[part]))
    for copy in copies:
        copy.wait()


VMEM = pl.BlockSpec(memory_space=pltpu.VMEM)
SMEM = pl.BlockSpec(memory_space=pltpu.SMEM)
ANY = pl.BlockSpec(memory_space=pl.ANY)


def call(body, outs, in_specs, args, scratch=(), out_specs=None, aliases=None, micros=0.0, name=None):
    return pl.pallas_call(
        body,
        out_shape=[x if hasattr(x, "dtype") else jax.ShapeDtypeStruct(x, F32) for x in outs],
        in_specs=in_specs,
        out_specs=out_specs or [VMEM] * len(outs),
        input_output_aliases=aliases or {},
        scratch_shapes=list(scratch),
        compiler_params=pltpu.CompilerParams(vmem_limit_bytes=24 * 1024 * 1024),
        cost_estimate=pl.CostEstimate(flops=int(micros * 1e9), bytes_accessed=1, transcendentals=0),
        name=name,
    )(*args)


def shards(object_field, probe, positions, residual, saved_wave):
    window = probe.shape[-1]
    half = window // 2
    count = positions.shape[0]
    size = notes_size(count)
    table = jnp.asarray(tables(window))
    barrier = lax.optimization_barrier

    def twice(*planes):
        return pltpu.VMEM((*planes, 2 * window + 8, window), F32)

    grads = pltpu.VMEM((2, count, window, window), F32)
    pos_scratch = [pltpu.SMEM(positions.shape, jnp.int32), pltpu.SemaphoreType.DMA]
    fields_shape = (count, 2, window, window)
    wide_shape = (2, window, 2 * window)
    square, strip = (2, half, window), (2, window, half)

    edge_first, edge_second = call(
        edges, [strip] * 2, [VMEM], (object_field,), micros=12.0, name="edges"
    )
    halo_first = swapped(edge_first, "gx", 0)
    halo_second = swapped(edge_second, "gx", 1)

    field, up2, down2, inner2_first, inner2_second, middle2, notes, marks = call(
        detect,
        [fields_shape]
        + [(4, half + size, window)] * 2
        + [square, square, wide_shape, (size, half), jax.ShapeDtypeStruct((2 * count, 8, window), jnp.int32)],
        [ANY] + [VMEM] * 4,
        (positions, residual, saved_wave, table, object_field),
        [twice(count, 2), grads] + pos_scratch,
        micros=12.0, name="detect",
    )
    from_down2 = swapped(down2, "gy", 1)
    from_up2 = swapped(up2, "gy", 0)

    fields, probes = call(
        roll_fields,
        [fields_shape] * 2,
        [ANY] + [VMEM] * 2,
        (positions, field, probe),
        [twice(count + 1, 2)] + pos_scratch,
        micros=0.1, name="roll",
    )
    rows_first, rows_second = call(
        relay,
        [square] * 2,
        [VMEM] * 2,
        (halo_first, halo_second),
        micros=12.0, name="widen",
    )
    from_rows_second = swapped(rows_second, "gy", 1)
    from_rows_first = swapped(rows_first, "gy", 0)

    from_down2, from_up2, fields, probes = barrier((from_down2, from_up2, fields, probes))
    first2, second2 = call(
        narrow_noted,
        [(2, window + 3 * size, half)] * 2,
        [VMEM] * 4,
        (notes, middle2, from_down2, from_up2),
        micros=0.2, name="narrow2",
    )
    from_rows_second, from_rows_first, marks, _ = barrier((from_rows_second, from_rows_first, marks, first2))
    got_first2 = swapped(first2, "gx", 0)
    got_second2 = swapped(second2, "gx", 1)

    outer_first, outer_second, inner_first, inner_second, middle1 = call(
        propagate,
        [square] * 2 + [(4, half, window)] * 2 + [wide_shape],
        [VMEM] * 13,
        (marks, fields, probes, object_field, halo_first, halo_second, from_down2, from_up2)
        + (from_rows_second, from_rows_first, table, inner2_first, inner2_second),
        [pltpu.VMEM(fields_shape, BF16)] * 2 + [grads],
        micros=0.1, name="propagate",
    )
    from_outer_second = swapped(outer_second, "gy", 1)
    from_outer_first = swapped(outer_first, "gy", 0)
    (total2_second,) = call(
        functools.partial(join, low=True), [strip], [VMEM] * 2, (middle2, got_second2), micros=1.0, name="join3"
    )
    (total2_first,) = call(
        functools.partial(join, low=False), [strip], [VMEM] * 2, (middle2, got_first2), micros=0.5, name="join2"
    )
    middle1, total2_first, total2_second = barrier((middle1, total2_first, total2_second))
    first1, second1_re, second1_im = call(
        narrow_parts,
        [strip] + [(1, window, half)] * 2,
        [VMEM] * 3,
        (middle1, from_outer_second, from_outer_first),
        [pltpu.VMEM(strip, F32)],
        micros=0.2, name="narrow1",
    )
    got_first1 = swapped(first1, "gx", 0)
    got_second1_im = around(second1_im, "gx")
    got_second1_re = swapped(second1_re, "gx", 1)
    from_inner_first = swapped(inner_first, "gy", 0)
    from_inner_second = swapped(inner_second, "gy", 1)

    (scale,) = call(
        illuminate,
        [(window, window)],
        [SMEM] + [VMEM] * 5,
        (positions, probe, from_up2, from_down2, got_first2, got_second2),
        [twice(), pltpu.SMEM((8 * size, half), F32), pltpu.SemaphoreType.DMA((4,))],
        micros=2.5, name="illuminate",
    )
    value = pltpu.VMEM(fields_shape[1:], F32)
    (begun,) = call(
        update_second,
        [object_field.shape],
        [VMEM] * 6,
        (object_field, scale, total2_first, total2_second, from_inner_second, from_inner_first),
        [value, pltpu.SemaphoreType.DMA],
        out_specs=[ANY], micros=0.1, name="update2",
    )
    (new_object,) = call(
        update_first,
        [object_field.shape],
        [ANY] + [VMEM] * 8,
        (begun, got_first1, got_second1_re, got_second1_im, object_field, scale, middle1)
        + (from_inner_second, from_inner_first),
        [value, pltpu.SemaphoreType.DMA((2,))],
        out_specs=[ANY], aliases={0: 0}, micros=1.0, name="update",
    )
    return new_object


def solution(mesh):
    placed = (
        P(None, None, "gy", "gx"),
        P(),
        P("gy", "gx", None),
        P("gy", "gx", None, None, None),
        P("gy", "gx", None, None, None),
    )
    return jax.shard_map(
        shards, mesh=mesh, in_specs=placed, out_specs=P(None, None, "gy", "gx"), check_vma=False
    )
```

```python
import functools

import jax
import jax.numpy as jnp
import ml_dtypes
import numpy as np
from jax import lax
from jax.experimental import pallas as pl
from jax.experimental.pallas import tpu as pltpu
from jax.sharding import PartitionSpec as P

fresnel_rate = 200.0
ridge = 0.5
CHUNK = 32
F32 = jnp.float32
BF16 = jnp.bfloat16


def two_parts(table):
    high = table.astype(np.float32).astype(ml_dtypes.bfloat16)
    low = (table - high.astype(np.float64)).astype(ml_dtypes.bfloat16)
    return high, low


@functools.lru_cache(maxsize=None)
def tables(size):
    index = np.arange(size)
    inverse = np.exp(2j * np.pi * (np.outer(index, index) % size) / size) / np.sqrt(size)
    freq = ((index + size // 2) % size - size // 2) / size
    move = inverse @ np.diag(np.exp(1j * fresnel_rate * freq**2)) @ inverse.conj()
    out = []
    for matrix in (inverse, move):
        out.extend(two_parts(np.concatenate([matrix.real, matrix.imag], axis=1)))
    return np.stack(out)


def swap_pairs(count, first):
    pairs = []
    for low in range(first, count - 1, 2):
        pairs += [(low, low + 1), (low + 1, low)]
    return pairs


def swapped(value, axis, first):
    return lax.ppermute(value, axis, swap_pairs(lax.axis_size(axis), first))


def around(value, axis):
    count = lax.axis_size(axis)
    if count % 2 or count < 4:
        return swapped(value, axis, 1)
    out, back = [], []
    for low in range(1, count - 1, 2):
        out += [(low, low + 2), (low + 1, low - 1)]
        back += [(low + 2, low + 1), (low - 1, low)]
    return lax.ppermute(lax.ppermute(value, axis, out), axis, back)


def dot(a, b):
    return jnp.dot(a, b, preferred_element_type=F32)


def split(value):
    high = value.astype(BF16)
    return high, (value - high.astype(F32)).astype(BF16)


def place(waves, corners, out_first, out_second, out_middle, odd, window):
    half = window // 2

    def rows(base, lower, store):
        for start in range(0, half, CHUNK):
            at = pl.multiple_of(base + start, CHUNK)
            row = lax.broadcasted_iota(jnp.int32, (CHUNK, window), 0) + at
            col = lax.broadcasted_iota(jnp.int32, (CHUNK, window), 1)
            masks = []
            for r, c in corners:
                inside = (row < r) == (lower == 1)
                masks.append((inside & (col >= c), inside & (col < c)))
            for plane in range(len(waves)):
                left = right = None
                for number, (in_left, in_right) in enumerate(masks):
                    value = waves[plane][number, pl.ds(at, CHUNK), :]
                    a = jnp.where(in_left, value, 0.0)
                    b = jnp.where(in_right, value, 0.0)
                    left = a if left is None else left + a
                    right = b if right is None else right + b
                store(plane, start, left, right)

    def writer(ref, offset):
        def store(plane, start, left, right):
            at = slice(offset + start, offset + start + CHUNK)
            if isinstance(ref, tuple):
                ref[0][plane, at, :half] = left[:, :half]
                ref[0][plane, at, half:] = right[:, half:]
                ref[1][plane, at, :half] = left[:, half:]
                ref[1][plane, at, half:] = right[:, :half]
            else:
                ref[plane, at, :window] = left
                ref[plane, at, window:] = right

        return store

    rows((1 - odd) * half, 1 - odd, writer(out_first, 0))
    rows(odd * half, odd, writer(out_second, 0))
    rows(half, 0, writer(out_middle, 0))
    rows(0, 1, writer(out_middle, half))


def from_right(rows_re, rows_im, high, low, passes):
    window = high.shape[0]
    sums = []
    for rows in (rows_re, rows_im):
        total = dot(rows[0], high[...]) + dot(rows[0], low[...])
        if passes == 3:
            total += dot(rows[1], high[...])
        sums.append(total)
    one, two = sums
    return one[:, :window] - two[:, window:], one[:, window:] + two[:, :window]


def from_left(high, low, inner_hi, inner_lo):
    window = high.shape[0]
    sums = []
    for part in range(2):
        cols = slice(part * window, (part + 1) * window)
        sums.append(dot(high[:, cols], inner_hi) + dot(low[:, cols], inner_hi) + dot(high[:, cols], inner_lo))
    one, two = sums
    return one[:, :window] - two[:, window:], one[:, window:] + two[:, :window]


def rolled(twice, corner, store, window):
    r, c = corner
    rest = lax.rem(window - r, 8)
    back = lax.rem(CHUNK + 8 - rest, CHUNK + 8)
    for start in range(0, window, CHUNK):
        value = twice[pl.ds(pl.multiple_of(window - r - rest + start, 8), CHUNK + 8), :]
        store(start, pltpu.roll(pltpu.roll(value, back, 0)[:CHUNK], c, 1))


def twofold(twice, start, value, window):
    rows = value.shape[0]
    twice[start : start + rows] = value
    twice[window + start : window + start + rows] = value
    if start == 0:
        twice[2 * window : 2 * window + 8] = value[:8]


def corners_of(pos):
    return [(pos[number, 0, 0], pos[number, 0, 1]) for number in range(pos.shape[0])]


def fetched(pos_any, pos, sem):
    copy = pltpu.make_async_copy(pos_any, pos, sem)
    copy.start()
    return copy


def detect(
    pos_any, residual, wave, table, object_field,
    field, first, second, inner_first, inner_second, middle, notes, marks,
    twice, grads, pos, sem,
):
    window = residual.shape[-1]
    count = residual.shape[0]
    odd = lax.rem(lax.axis_index("gy"), 2)
    arrival = fetched(pos_any, pos, sem)
    table_hi, table_lo = table.at[0], table.at[1]
    for number in range(count):
        line = from_right((residual[number, 0, 0],), (residual[number, 0, 1],), table_hi, table_lo, 2)
        high, low = split(jnp.concatenate(line, axis=1))
        field_re, field_im = from_left(table_hi, table_lo, high, low)
        field[number, 0] = field_re
        field[number, 1] = field_im
        for start in range(0, window, CHUNK):
            rows = slice(start, start + CHUNK)
            wave_re, wave_im = wave[number, 0, 0, rows].astype(F32), wave[number, 0, 1, rows].astype(F32)
            value_re, value_im = field[number, 0, rows], field[number, 1, rows]
            twofold(twice.at[number, 0], start, wave_re * value_re + wave_im * value_im, window)
            twofold(twice.at[number, 1], start, wave_re * value_im - wave_im * value_re, window)
    arrival.wait()
    corners = corners_of(pos)
    for number, corner in enumerate(corners):
        for part in range(2):

            def store(start, value):
                grads[part, number, start : start + CHUNK] = value

            rolled(twice.at[number, part], corner, store, window)
            marks[2 * number + part] = jnp.full(marks.shape[1:], corner[part], jnp.int32)
    place([grads.at[0], grads.at[1]], corners, (first, inner_first), (second, inner_second), middle, odd, window)
    half = window // 2
    for ref, base in ((first, (1 - odd) * half), (second, odd * half)):
        ref[0, half:] = notes_of(pos, count, window)
        for part in range(2):
            ref[2 + part, :half] = object_field[1, part, pl.ds(pl.multiple_of(base, half), half), :]
    notes[...] = notes_of(pos, count, window // 2)


def roll_fields(pos_any, field, probe, field_out, probes, twice, pos, sem):
    window = probe.shape[-1]
    count = field.shape[0]
    arrival = fetched(pos_any, pos, sem)
    for part in range(2):
        for start in range(0, window, CHUNK):
            twofold(twice.at[count, part], start, probe[part, start : start + CHUNK], window)
            for number in range(count):
                twofold(twice.at[number, part], start, field[number, part, start : start + CHUNK], window)
    arrival.wait()
    for number, corner in enumerate(corners_of(pos)):
        for part in range(2):

            def to_field(start, value):
                field_out[number, part, start : start + CHUNK] = value

            rolled(twice.at[number, part], corner, to_field, window)

            def to_probes(start, value):
                probes[number, part, start : start + CHUNK] = value

            rolled(twice.at[count, part], corner, to_probes, window)


def notes_size(count):
    return -(-(1 + 2 * count) // 8) * 8


def notes_of(pos, count, width):
    size = notes_size(count)
    row = lax.broadcasted_iota(jnp.int32, (size, width), 0)
    notes = jnp.where(row == 0, 1, 0)
    for number in range(count):
        for part in range(2):
            notes = jnp.where(row == 1 + 2 * number + part, pos[number, 0, part], notes)
    return notes.astype(F32)


def sides(odd, one, two):
    return jnp.where(odd == 1, one, two), jnp.where(odd == 1, two, one)


def edges(object_field, first, second):
    half = object_field.shape[-1] // 2
    odd_x = lax.rem(lax.axis_index("gx"), 2)
    for ref, odd in ((first, 1 - odd_x), (second, odd_x)):
        ref[...] = object_field[1, :, :, pl.ds(pl.multiple_of(odd * half, half), half)]


def relay(from_first, from_second, first, second):
    half = from_first.shape[-1]
    odd_x = lax.rem(lax.axis_index("gx"), 2)
    odd_y = lax.rem(lax.axis_index("gy"), 2)
    at_first = pl.ds(pl.multiple_of((1 - odd_x) * half, half), half)
    at_second = pl.ds(pl.multiple_of(odd_x * half, half), half)
    for ref, base in ((first, (1 - odd_y) * half), (second, odd_y * half)):
        rows = pl.ds(pl.multiple_of(base, half), half)
        for plane in range(ref.shape[0]):
            ref[plane, :, at_first] = from_first[plane, rows]
            ref[plane, :, at_second] = from_second[plane, rows]


def propagate(
    marks, field, probes, object_field, halo_first, halo_second,
    own_second, own_first, corner_second, corner_first, table, inner2_first, inner2_second,
    outer_first, outer_second, inner_first, inner_second, middle,
    chi_hi, chi_lo, grads,
):
    window = field.shape[-1]
    half = window // 2
    count = field.shape[0]
    odd_x = lax.rem(lax.axis_index("gx"), 2)
    odd = lax.rem(lax.axis_index("gy"), 2)
    corners = [(marks[2 * number, :1], marks[2 * number + 1, :1]) for number in range(count)]
    table_hi, table_lo = table.at[2], table.at[3]
    inner_first[2:] = inner2_first[...]
    inner_second[2:] = inner2_second[...]

    def wide(part, rows):
        left, right = sides(odd_x, halo_first[part, rows], halo_second[part, rows])
        return jnp.concatenate([left, object_field[1, part, rows], right], axis=1)

    def beyond(part, rows, below):
        own = sides(odd, own_first[2 + part, rows], own_second[2 + part, rows])[below]
        corner = sides(odd, corner_first[part, rows], corner_second[part, rows])[below]
        return jnp.concatenate([corner[:, :half], own, corner[:, half:]], axis=1)

    for start in range(0, window, CHUNK):
        rows = slice(start, start + CHUNK)
        row = lax.broadcasted_iota(jnp.int32, (CHUNK, window), 0) + start
        col = lax.broadcasted_iota(jnp.int32, (CHUNK, window), 1)
        upper, lower = [], []
        for part in range(2):
            if start < half:
                upper.append(beyond(part, rows, 0))
                lower.append(wide(part, slice(half + start, half + start + CHUNK)))
            else:
                shifted = slice(start - half, start - half + CHUNK)
                upper.append(wide(part, shifted))
                lower.append(beyond(part, shifted, 1))
        for number, (r, c) in enumerate(corners):
            low_row, low_col = row < r, col < c
            patch = []
            for part in range(2):
                above = jnp.where(low_col, upper[part][:, window:], upper[part][:, :window])
                below = jnp.where(low_col, lower[part][:, window:], lower[part][:, :window])
                patch.append(jnp.where(low_row, below, above))
            field_re, field_im = field[number, 0, rows], field[number, 1, rows]
            high, low = split(patch[0] * field_re + patch[1] * field_im)
            chi_hi[number, 0, rows] = high
            chi_lo[number, 0, rows] = low
            high, low = split(patch[0] * field_im - patch[1] * field_re)
            chi_hi[number, 1, rows] = high
            chi_lo[number, 1, rows] = low

    for number in range(count):
        line = from_right(
            (chi_hi[number, 0], chi_lo[number, 0]), (chi_hi[number, 1], chi_lo[number, 1]), table_hi, table_lo, 3
        )
        high, low = split(jnp.concatenate(line, axis=1))
        back_re, back_im = from_left(table_hi, table_lo, high, low)
        probe_re, probe_im = probes[number, 0], probes[number, 1]
        grads[0, number] = probe_re * back_re + probe_im * back_im
        grads[1, number] = probe_re * back_im - probe_im * back_re
    place(
        [grads.at[0], grads.at[1]], corners, (outer_first, inner_first), (outer_second, inner_second), middle, odd, window
    )


def illuminate(pos, probe, up, down, first, second, scale, twice, notes, sems):
    window = probe.shape[-1]
    half = window // 2
    count = pos.shape[0]
    size = notes_size(count)
    odd_x = lax.rem(lax.axis_index("gx"), 2)
    odd_y = lax.rem(lax.axis_index("gy"), 2)
    copies, at = [], 0
    for ref, start, rows in ((up, half, size), (down, half, size), (first, window, 3 * size), (second, window, 3 * size)):
        source = ref.at[0, pl.ds(start, rows), pl.ds(0, half)]
        copies.append(pltpu.make_async_copy(source, notes.at[pl.ds(at, rows), :], sems.at[len(copies)]))
        copies[-1].start()
        at += rows
    for start in range(0, window, CHUNK):
        rows = slice(start, start + CHUNK)
        twofold(twice, start, probe[0, rows] * probe[0, rows] + probe[1, rows] * probe[1, rows], window)
    for copy in copies:
        copy.wait()

    upper, lower = [], []
    for down in (-1, 0, 1):
        for along in (-1, 0, 1):
            if along == 0:
                base = (odd_y if down > 0 else 1 - odd_y) * size
            else:
                base = (2 + 3 * (odd_x if along > 0 else 1 - odd_x) + 1 + down) * size
            for number in range(count):
                if down == 0 and along == 0:
                    valid, r, c = 1, pos[number, 0, 0], pos[number, 0, 1]
                else:
                    valid, r, c = (
                        notes[base + row, 0].astype(jnp.int32) for row in (0, 1 + 2 * number, 2 + 2 * number)
                    )
                top = r - half + window * down
                left = c - half + window * along
                top = jnp.where(valid == 1, top, window)
                for reached, half_at in ((upper, -1), (lower, 1)):
                    if down in (0, half_at):
                        reached.append((top, left, r, c))

    def rows_at(index, carry, shifts):
        start = index * CHUNK
        row = lax.broadcasted_iota(jnp.int32, (CHUNK, window), 0) + start
        col = lax.broadcasted_iota(jnp.int32, (CHUNK, window), 1)
        here = pl.ds(pl.multiple_of(start, CHUNK), CHUNK)
        scale[here, :] = jnp.zeros((CHUNK, window), F32)
        for top, left, r, c in shifts:

            @pl.when((top < start + CHUNK) & (top + window > start) & (left < window) & (left + window > 0))
            def _():
                turn = lax.rem(2 * window - half - r, window)
                rest = lax.rem(turn, 8)
                value = twice[pl.ds(pl.multiple_of(turn - rest + start, 8), CHUNK + 8), :]
                value = pltpu.roll(value, lax.rem(CHUNK + 8 - rest, CHUNK + 8), 0)[:CHUNK]
                value = pltpu.roll(value, lax.rem(c + half, window), 1)
                inside = (row >= top) & (row < top + window) & (col >= left) & (col < left + window)
                scale[here, :] += jnp.where(inside, value, 0.0)

        scale[here, :] = 1.0 / (scale[here, :] + ridge)
        return carry

    lax.fori_loop(0, half // CHUNK, functools.partial(rows_at, shifts=upper), 0)
    lax.fori_loop(half // CHUNK, window // CHUNK, functools.partial(rows_at, shifts=lower), 0)


def narrow_noted(notes, middle, from_second, from_first, first, second):
    half = first.shape[-1]
    window = 2 * half
    odd_y = lax.rem(lax.axis_index("gy"), 2)
    columns = pl.ds(0, window)
    narrow_outer(
        middle, from_second.at[:2, :half], from_first.at[:2, :half], first.at[:, columns], second.at[:, columns]
    )
    size = notes.shape[0]
    above, below = sides(odd_y, from_first[0, half:, :half], from_second[0, half:, :half])
    for ref in (first, second):
        ref[0, window : window + size] = above
        ref[0, window + size : window + 2 * size] = notes[...]
        ref[0, window + 2 * size :] = below


def narrow_parts(middle, from_second, from_first, first, second_re, second_im, second):
    narrow_outer(middle, from_second, from_first, first, second)
    second_re[0] = second[0]
    second_im[0] = second[1]


def narrow_outer(middle, from_second, from_first, first, second):
    half = first.shape[-1]
    odd_x = lax.rem(lax.axis_index("gx"), 2)
    odd_y = lax.rem(lax.axis_index("gy"), 2)
    for plane in range(middle.shape[0]):
        for received, base in ((from_first, (1 - odd_y) * half), (from_second, odd_y * half)):
            at = pl.ds(pl.multiple_of(base, half), half)
            left = middle[plane, at, :half] + received[plane, :, :half]
            right = middle[plane, at, 3 * half :] + received[plane, :, half:]
            second[plane, at, :], first[plane, at, :] = sides(odd_x, right, left)


def join(middle, received, out, low):
    window = middle.shape[1]
    half = window // 2
    odd_x = lax.rem(lax.axis_index("gx"), 2)
    base = (odd_x if low else 1 - odd_x) * half
    at = pl.ds(pl.multiple_of(half + base, half), half)
    out[...] = middle[:, :, at] + received[:, :window]


def written(value, out, number, sem):
    copy = pltpu.make_async_copy(value, out.at[number], sem)
    copy.start()
    return copy


def update_second(
    object_field, scale, total2_first, total2_second, inner_second, inner_first, out, value, sem
):
    half = scale.shape[-1] // 2
    odd_x = lax.rem(lax.axis_index("gx"), 2)
    odd_y = lax.rem(lax.axis_index("gy"), 2)
    for part in range(2):
        for received, base in ((inner_first, (1 - odd_y) * half), (inner_second, odd_y * half)):
            rows = pl.ds(pl.multiple_of(base, half), half)
            outer = jnp.concatenate(sides(odd_x, total2_first[part, rows], total2_second[part, rows]), axis=1)
            value[part, rows] = object_field[1, part, rows] - (outer + received[2 + part]) * scale[rows]
    written(value, out, 1, sem).wait()


def update_first(
    begun, first1, second1_re, second1_im, object_field, scale, middle1, inner_second, inner_first, out, value, sems
):
    del begun
    window = scale.shape[-1]
    half = window // 2
    odd_x = lax.rem(lax.axis_index("gx"), 2)
    odd_y = lax.rem(lax.axis_index("gy"), 2)
    copies = []
    for part in range(2):
        for received, base in ((inner_first, (1 - odd_y) * half), (inner_second, odd_y * half)):
            rows = pl.ds(pl.multiple_of(base, half), half)
            outer = jnp.concatenate(sides(odd_x, first1[part, rows], (second1_re, second1_im)[part][0, rows]), axis=1)
            total = middle1[part, rows, half : 3 * half] + received[part] + outer
            value[part, rows] = object_field[0, part, rows] - total * scale[rows]
        copies.append(written(value.at[part], out.at[0], part, sems.at[part]))
    for copy in copies:
        copy.wait()


VMEM = pl.BlockSpec(memory_space=pltpu.VMEM)
SMEM = pl.BlockSpec(memory_space=pltpu.SMEM)
ANY = pl.BlockSpec(memory_space=pl.ANY)


def call(body, outs, in_specs, args, scratch=(), out_specs=None, aliases=None, micros=0.0, name=None):
    return pl.pallas_call(
        body,
        out_shape=[x if hasattr(x, "dtype") else jax.ShapeDtypeStruct(x, F32) for x in outs],
        in_specs=in_specs,
        out_specs=out_specs or [VMEM] * len(outs),
        input_output_aliases=aliases or {},
        scratch_shapes=list(scratch),
        compiler_params=pltpu.CompilerParams(vmem_limit_bytes=24 * 1024 * 1024),
        cost_estimate=pl.CostEstimate(flops=int(micros * 1e9), bytes_accessed=1, transcendentals=0),
        name=name,
    )(*args)


def shards(object_field, probe, positions, residual, saved_wave):
    window = probe.shape[-1]
    half = window // 2
    count = positions.shape[0]
    size = notes_size(count)
    table = jnp.asarray(tables(window))
    barrier = lax.optimization_barrier

    def twice(*planes):
        return pltpu.VMEM((*planes, 2 * window + 8, window), F32)

    grads = pltpu.VMEM((2, count, window, window), F32)
    pos_scratch = [pltpu.SMEM(positions.shape, jnp.int32), pltpu.SemaphoreType.DMA]
    fields_shape = (count, 2, window, window)
    wide_shape = (2, window, 2 * window)
    square, strip = (2, half, window), (2, window, half)

    edge_first, edge_second = call(
        edges, [strip] * 2, [VMEM], (object_field,), micros=12.0, name="edges"
    )
    halo_first = swapped(edge_first, "gx", 0)
    halo_second = swapped(edge_second, "gx", 1)

    field, up2, down2, inner2_first, inner2_second, middle2, notes, marks = call(
        detect,
        [fields_shape]
        + [(4, half + size, window)] * 2
        + [square, square, wide_shape, (size, half), jax.ShapeDtypeStruct((2 * count, 8, window), jnp.int32)],
        [ANY] + [VMEM] * 4,
        (positions, residual, saved_wave, table, object_field),
        [twice(count, 2), grads] + pos_scratch,
        micros=12.0, name="detect",
    )
    from_down2 = swapped(down2, "gy", 1)
    from_up2 = swapped(up2, "gy", 0)

    fields, probes = call(
        roll_fields,
        [fields_shape] * 2,
        [ANY] + [VMEM] * 2,
        (positions, field, probe),
        [twice(count + 1, 2)] + pos_scratch,
        micros=0.1, name="roll",
    )
    rows_first, rows_second = call(
        relay,
        [square] * 2,
        [VMEM] * 2,
        (halo_first, halo_second),
        micros=12.0, name="widen",
    )
    from_rows_second = swapped(rows_second, "gy", 1)
    from_rows_first = swapped(rows_first, "gy", 0)

    from_down2, from_up2, fields, probes = barrier((from_down2, from_up2, fields, probes))
    first2, second2 = call(
        narrow_noted,
        [(2, window + 3 * size, half)] * 2,
        [VMEM] * 4,
        (notes, middle2, from_down2, from_up2),
        micros=0.2, name="narrow2",
    )
    from_rows_second, from_rows_first, marks, _ = barrier((from_rows_second, from_rows_first, marks, first2))
    got_first2 = swapped(first2, "gx", 0)
    got_second2 = swapped(second2, "gx", 1)

    outer_first, outer_second, inner_first, inner_second, middle1 = call(
        propagate,
        [square] * 2 + [(4, half, window)] * 2 + [wide_shape],
        [VMEM] * 13,
        (marks, fields, probes, object_field, halo_first, halo_second, from_down2, from_up2)
        + (from_rows_second, from_rows_first, table, inner2_first, inner2_second),
        [pltpu.VMEM(fields_shape, BF16)] * 2 + [grads],
        micros=0.1, name="propagate",
    )
    from_outer_second = swapped(outer_second, "gy", 1)
    from_outer_first = swapped(outer_first, "gy", 0)
    (total2_second,) = call(
        functools.partial(join, low=True), [strip], [VMEM] * 2, (middle2, got_second2), micros=1.0, name="join3"
    )
    (total2_first,) = call(
        functools.partial(join, low=False), [strip], [VMEM] * 2, (middle2, got_first2), micros=0.5, name="join2"
    )
    middle1, total2_first, total2_second = barrier((middle1, total2_first, total2_second))
    first1, second1_re, second1_im = call(
        narrow_parts,
        [strip] + [(1, window, half)] * 2,
        [VMEM] * 3,
        (middle1, from_outer_second, from_outer_first),
        [pltpu.VMEM(strip, F32)],
        micros=0.2, name="narrow1",
    )
    got_first1 = swapped(first1, "gx", 0)
    got_second1_im = around(second1_im, "gx")
    got_second1_re = swapped(second1_re, "gx", 1)
    from_inner_first = swapped(inner_first, "gy", 0)
    from_inner_second = swapped(inner_second, "gy", 1)

    (scale,) = call(
        illuminate,
        [(window, window)],
        [SMEM] + [VMEM] * 5,
        (positions, probe, from_up2, from_down2, got_first2, got_second2),
        [twice(), pltpu.SMEM((8 * size, half), F32), pltpu.SemaphoreType.DMA((4,))],
        micros=2.5, name="illuminate",
    )
    value = pltpu.VMEM(fields_shape[1:], F32)
    (begun,) = call(
        update_second,
        [object_field.shape],
        [VMEM] * 6,
        (object_field, scale, total2_first, total2_second, from_inner_second, from_inner_first),
        [value, pltpu.SemaphoreType.DMA],
        out_specs=[ANY], micros=0.1, name="update2",
    )
    (new_object,) = call(
        update_first,
        [object_field.shape],
        [ANY] + [VMEM] * 8,
        (begun, got_first1, got_second1_re, got_second1_im, object_field, scale, middle1)
        + (from_inner_second, from_inner_first),
        [value, pltpu.SemaphoreType.DMA((2,))],
        out_specs=[ANY], aliases={0: 0}, micros=1.0, name="update",
    )
    return new_object


def solution(mesh):
    placed = (
        P(None, None, "gy", "gx"),
        P(),
        P("gy", "gx", None),
        P("gy", "gx", None, None, None),
        P("gy", "gx", None, None, None),
    )
    return jax.shard_map(
        shards, mesh=mesh, in_specs=placed, out_specs=P(None, None, "gy", "gx"), check_vma=False
    )
```

```python
import functools

import jax
import jax.numpy as jnp
import ml_dtypes
import numpy as np
from jax import lax
from jax.experimental import pallas as pl
from jax.experimental.pallas import tpu as pltpu
from jax.sharding import PartitionSpec as P

fresnel_rate = 200.0
ridge = 0.5
CHUNK = 32
F32 = jnp.float32
BF16 = jnp.bfloat16


def two_parts(table):
    high = table.astype(np.float32).astype(ml_dtypes.bfloat16)
    low = (table - high.astype(np.float64)).astype(ml_dtypes.bfloat16)
    return high, low


@functools.lru_cache(maxsize=None)
def tables(size):
    index = np.arange(size)
    inverse = np.exp(2j * np.pi * (np.outer(index, index) % size) / size) / np.sqrt(size)
    freq = ((index + size // 2) % size - size // 2) / size
    move = inverse @ np.diag(np.exp(1j * fresnel_rate * freq**2)) @ inverse.conj()
    out = []
    for matrix in (inverse, move):
        out.extend(two_parts(np.concatenate([matrix.real, matrix.imag], axis=1)))
    return np.stack(out)


def swap_pairs(count, first):
    pairs = []
    for low in range(first, count - 1, 2):
        pairs += [(low, low + 1), (low + 1, low)]
    return pairs


def swapped(value, axis, first):
    return lax.ppermute(value, axis, swap_pairs(lax.axis_size(axis), first))


def around(value, axis):
    count = lax.axis_size(axis)
    if count % 2 or count < 4:
        return swapped(value, axis, 1)
    out, back = [], []
    for low in range(1, count - 1, 2):
        out += [(low, low + 2), (low + 1, low - 1)]
        back += [(low + 2, low + 1), (low - 1, low)]
    return lax.ppermute(lax.ppermute(value, axis, out), axis, back)


def dot(a, b):
    return jnp.dot(a, b, preferred_element_type=F32)


def split(value):
    high = value.astype(BF16)
    return high, (value - high.astype(F32)).astype(BF16)


def place(waves, corners, out_first, out_second, out_middle, odd, window):
    half = window // 2

    def rows(base, lower, store):
        for start in range(0, half, CHUNK):
            at = pl.multiple_of(base + start, CHUNK)
            row = lax.broadcasted_iota(jnp.int32, (CHUNK, window), 0) + at
            col = lax.broadcasted_iota(jnp.int32, (CHUNK, window), 1)
            masks = []
            for r, c in corners:
                inside = (row < r) == (lower == 1)
                masks.append((inside & (col >= c), inside & (col < c)))
            for plane in range(len(waves)):
                left = right = None
                for number, (in_left, in_right) in enumerate(masks):
                    value = waves[plane][number, pl.ds(at, CHUNK), :]
                    a = jnp.where(in_left, value, 0.0)
                    b = jnp.where(in_right, value, 0.0)
                    left = a if left is None else left + a
                    right = b if right is None else right + b
                store(plane, start, left, right)

    def writer(ref, offset):
        def store(plane, start, left, right):
            at = slice(offset + start, offset + start + CHUNK)
            if isinstance(ref, tuple):
                ref[0][plane, at, :half] = left[:, :half]
                ref[0][plane, at, half:] = right[:, half:]
                ref[1][plane, at, :half] = left[:, half:]
                ref[1][plane, at, half:] = right[:, :half]
            else:
                ref[plane, at, :window] = left
                ref[plane, at, window:] = right

        return store

    rows((1 - odd) * half, 1 - odd, writer(out_first, 0))
    rows(odd * half, odd, writer(out_second, 0))
    rows(half, 0, writer(out_middle, 0))
    rows(0, 1, writer(out_middle, half))


def from_right(rows_re, rows_im, high, low, passes):
    window = high.shape[0]
    sums = []
    for rows in (rows_re, rows_im):
        total = dot(rows[0], high[...]) + dot(rows[0], low[...])
        if passes == 3:
            total += dot(rows[1], high[...])
        sums.append(total)
    one, two = sums
    return one[:, :window] - two[:, window:], one[:, window:] + two[:, :window]


def from_left(high, low, inner_hi, inner_lo):
    window = high.shape[0]
    sums = []
    for part in range(2):
        cols = slice(part * window, (part + 1) * window)
        sums.append(dot(high[:, cols], inner_hi) + dot(low[:, cols], inner_hi) + dot(high[:, cols], inner_lo))
    one, two = sums
    return one[:, :window] - two[:, window:], one[:, window:] + two[:, :window]


def rolled(twice, corner, store, window):
    r, c = corner
    rest = lax.rem(window - r, 8)
    back = lax.rem(CHUNK + 8 - rest, CHUNK + 8)
    for start in range(0, window, CHUNK):
        value = twice[pl.ds(pl.multiple_of(window - r - rest + start, 8), CHUNK + 8), :]
        store(start, pltpu.roll(pltpu.roll(value, back, 0)[:CHUNK], c, 1))


def twofold(twice, start, value, window):
    rows = value.shape[0]
    twice[start : start + rows] = value
    twice[window + start : window + start + rows] = value
    if start == 0:
        twice[2 * window : 2 * window + 8] = value[:8]


def corners_of(pos):
    return [(pos[number, 0, 0], pos[number, 0, 1]) for number in range(pos.shape[0])]


def fetched(pos_any, pos, sem):
    copy = pltpu.make_async_copy(pos_any, pos, sem)
    copy.start()
    return copy


def detect(
    pos_any, residual, wave, table, object_field,
    field, first, second, inner_first, inner_second, middle, notes, marks,
    twice, grads, pos, sem,
):
    window = residual.shape[-1]
    count = residual.shape[0]
    odd = lax.rem(lax.axis_index("gy"), 2)
    arrival = fetched(pos_any, pos, sem)
    table_hi, table_lo = table.at[0], table.at[1]
    for number in range(count):
        line = from_right((residual[number, 0, 0],), (residual[number, 0, 1],), table_hi, table_lo, 2)
        high, low = split(jnp.concatenate(line, axis=1))
        field_re, field_im = from_left(table_hi, table_lo, high, low)
        field[number, 0] = field_re
        field[number, 1] = field_im
        for start in range(0, window, CHUNK):
            rows = slice(start, start + CHUNK)
            wave_re, wave_im = wave[number, 0, 0, rows].astype(F32), wave[number, 0, 1, rows].astype(F32)
            value_re, value_im = field[number, 0, rows], field[number, 1, rows]
            twofold(twice.at[number, 0], start, wave_re * value_re + wave_im * value_im, window)
            twofold(twice.at[number, 1], start, wave_re * value_im - wave_im * value_re, window)
    arrival.wait()
    corners = corners_of(pos)
    for number, corner in enumerate(corners):
        for part in range(2):

            def store(start, value):
                grads[part, number, start : start + CHUNK] = value

            rolled(twice.at[number, part], corner, store, window)
            marks[2 * number + part] = jnp.full(marks.shape[1:], corner[part], jnp.int32)
    place([grads.at[0], grads.at[1]], corners, (first, inner_first), (second, inner_second), middle, odd, window)
    half = window // 2
    for ref, base in ((first, (1 - odd) * half), (second, odd * half)):
        ref[0, half:] = notes_of(pos, count, window)
        for part in range(2):
            ref[2 + part, :half] = object_field[1, part, pl.ds(pl.multiple_of(base, half), half), :]
    notes[...] = notes_of(pos, count, window // 2)


def roll_fields(pos_any, field, probe, field_out, probes, twice, pos, sem):
    window = probe.shape[-1]
    count = field.shape[0]
    arrival = fetched(pos_any, pos, sem)
    for part in range(2):
        for start in range(0, window, CHUNK):
            twofold(twice.at[count, part], start, probe[part, start : start + CHUNK], window)
            for number in range(count):
                twofold(twice.at[number, part], start, field[number, part, start : start + CHUNK], window)
    arrival.wait()
    for number, corner in enumerate(corners_of(pos)):
        for part in range(2):

            def to_field(start, value):
                field_out[number, part, start : start + CHUNK] = value

            rolled(twice.at[number, part], corner, to_field, window)

            def to_probes(start, value):
                probes[number, part, start : start + CHUNK] = value

            rolled(twice.at[count, part], corner, to_probes, window)


def notes_size(count):
    return -(-(1 + 2 * count) // 8) * 8


def notes_of(pos, count, width):
    size = notes_size(count)
    row = lax.broadcasted_iota(jnp.int32, (size, width), 0)
    notes = jnp.where(row == 0, 1, 0)
    for number in range(count):
        for part in range(2):
            notes = jnp.where(row == 1 + 2 * number + part, pos[number, 0, part], notes)
    return notes.astype(F32)


def sides(odd, one, two):
    return jnp.where(odd == 1, one, two), jnp.where(odd == 1, two, one)


def edges(object_field, first, second):
    half = object_field.shape[-1] // 2
    odd_x = lax.rem(lax.axis_index("gx"), 2)
    for ref, odd in ((first, 1 - odd_x), (second, odd_x)):
        ref[...] = object_field[1, :, :, pl.ds(pl.multiple_of(odd * half, half), half)]


def relay(from_first, from_second, first, second):
    half = from_first.shape[-1]
    odd_x = lax.rem(lax.axis_index("gx"), 2)
    odd_y = lax.rem(lax.axis_index("gy"), 2)
    at_first = pl.ds(pl.multiple_of((1 - odd_x) * half, half), half)
    at_second = pl.ds(pl.multiple_of(odd_x * half, half), half)
    for ref, base in ((first, (1 - odd_y) * half), (second, odd_y * half)):
        rows = pl.ds(pl.multiple_of(base, half), half)
        for plane in range(ref.shape[0]):
            ref[plane, :, at_first] = from_first[plane, rows]
            ref[plane, :, at_second] = from_second[plane, rows]


def propagate(
    marks, field, probes, object_field, halo_first, halo_second,
    own_second, own_first, corner_second, corner_first, table, inner2_first, inner2_second,
    outer_first, outer_second, inner_first, inner_second, middle,
    chi_hi, chi_lo, grads,
):
    window = field.shape[-1]
    half = window // 2
    count = field.shape[0]
    odd_x = lax.rem(lax.axis_index("gx"), 2)
    odd = lax.rem(lax.axis_index("gy"), 2)
    corners = [(marks[2 * number, :1], marks[2 * number + 1, :1]) for number in range(count)]
    table_hi, table_lo = table.at[2], table.at[3]
    inner_first[2:] = inner2_first[...]
    inner_second[2:] = inner2_second[...]

    def wide(part, rows):
        left, right = sides(odd_x, halo_first[part, rows], halo_second[part, rows])
        return jnp.concatenate([left, object_field[1, part, rows], right], axis=1)

    def beyond(part, rows, below):
        own = sides(odd, own_first[2 + part, rows], own_second[2 + part, rows])[below]
        corner = sides(odd, corner_first[part, rows], corner_second[part, rows])[below]
        return jnp.concatenate([corner[:, :half], own, corner[:, half:]], axis=1)

    for start in range(0, window, CHUNK):
        rows = slice(start, start + CHUNK)
        row = lax.broadcasted_iota(jnp.int32, (CHUNK, window), 0) + start
        col = lax.broadcasted_iota(jnp.int32, (CHUNK, window), 1)
        upper, lower = [], []
        for part in range(2):
            if start < half:
                upper.append(beyond(part, rows, 0))
                lower.append(wide(part, slice(half + start, half + start + CHUNK)))
            else:
                shifted = slice(start - half, start - half + CHUNK)
                upper.append(wide(part, shifted))
                lower.append(beyond(part, shifted, 1))
        for number, (r, c) in enumerate(corners):
            low_row, low_col = row < r, col < c
            patch = []
            for part in range(2):
                above = jnp.where(low_col, upper[part][:, window:], upper[part][:, :window])
                below = jnp.where(low_col, lower[part][:, window:], lower[part][:, :window])
                patch.append(jnp.where(low_row, below, above))
            field_re, field_im = field[number, 0, rows], field[number, 1, rows]
            high, low = split(patch[0] * field_re + patch[1] * field_im)
            chi_hi[number, 0, rows] = high
            chi_lo[number, 0, rows] = low
            high, low = split(patch[0] * field_im - patch[1] * field_re)
            chi_hi[number, 1, rows] = high
            chi_lo[number, 1, rows] = low

    for number in range(count):
        line = from_right(
            (chi_hi[number, 0], chi_lo[number, 0]), (chi_hi[number, 1], chi_lo[number, 1]), table_hi, table_lo, 3
        )
        high, low = split(jnp.concatenate(line, axis=1))
        back_re, back_im = from_left(table_hi, table_lo, high, low)
        probe_re, probe_im = probes[number, 0], probes[number, 1]
        grads[0, number] = probe_re * back_re + probe_im * back_im
        grads[1, number] = probe_re * back_im - probe_im * back_re
    place(
        [grads.at[0], grads.at[1]], corners, (outer_first, inner_first), (outer_second, inner_second), middle, odd, window
    )


def illuminate(pos, probe, up, down, first, second, scale, twice, notes, sems):
    window = probe.shape[-1]
    half = window // 2
    count = pos.shape[0]
    size = notes_size(count)
    odd_x = lax.rem(lax.axis_index("gx"), 2)
    odd_y = lax.rem(lax.axis_index("gy"), 2)
    copies, at = [], 0
    for ref, start, rows in ((up, half, size), (down, half, size), (first, window, 3 * size), (second, window, 3 * size)):
        source = ref.at[0, pl.ds(start, rows), pl.ds(0, half)]
        copies.append(pltpu.make_async_copy(source, notes.at[pl.ds(at, rows), :], sems.at[len(copies)]))
        copies[-1].start()
        at += rows
    for start in range(0, window, CHUNK):
        rows = slice(start, start + CHUNK)
        twofold(twice, start, probe[0, rows] * probe[0, rows] + probe[1, rows] * probe[1, rows], window)
    for copy in copies:
        copy.wait()

    upper, lower = [], []
    for down in (-1, 0, 1):
        for along in (-1, 0, 1):
            if along == 0:
                base = (odd_y if down > 0 else 1 - odd_y) * size
            else:
                base = (2 + 3 * (odd_x if along > 0 else 1 - odd_x) + 1 + down) * size
            for number in range(count):
                if down == 0 and along == 0:
                    valid, r, c = 1, pos[number, 0, 0], pos[number, 0, 1]
                else:
                    valid, r, c = (
                        notes[base + row, 0].astype(jnp.int32) for row in (0, 1 + 2 * number, 2 + 2 * number)
                    )
                top = r - half + window * down
                left = c - half + window * along
                top = jnp.where(valid == 1, top, window)
                for reached, half_at in ((upper, -1), (lower, 1)):
                    if down in (0, half_at):
                        reached.append((top, left, r, c, along))

    def rows_at(index, carry, shifts):
        start = index * CHUNK
        row = lax.broadcasted_iota(jnp.int32, (CHUNK, window), 0) + start
        col = lax.broadcasted_iota(jnp.int32, (CHUNK, window), 1)
        totals = [jnp.zeros((CHUNK, half), F32)] * 2
        for top, left, r, c, along in shifts:
            turn = lax.rem(2 * window - half - r, window)
            rest = lax.rem(turn, 8)
            value = twice[pl.ds(pl.multiple_of(turn - rest + start, 8), CHUNK + 8), :]
            value = pltpu.roll(value, lax.rem(CHUNK + 8 - rest, CHUNK + 8), 0)[:CHUNK]
            value = pltpu.roll(value, lax.rem(c + half, window), 1)
            for side in range(2):
                if along == (1, -1)[side]:
                    continue
                cols = slice(side * half, (side + 1) * half)
                inside = (row[:, cols] >= top) & (row[:, cols] < top + window)
                inside &= (col[:, cols] >= left) & (col[:, cols] < left + window)
                totals[side] += jnp.where(inside, value[:, cols], 0.0)
        total = jnp.concatenate(totals, axis=1)
        scale[pl.ds(pl.multiple_of(start, CHUNK), CHUNK), :] = 1.0 / (total + ridge)
        return carry

    lax.fori_loop(0, half // CHUNK, functools.partial(rows_at, shifts=upper), 0)
    lax.fori_loop(half // CHUNK, window // CHUNK, functools.partial(rows_at, shifts=lower), 0)


def narrow_noted(notes, middle, from_second, from_first, first, second):
    half = first.shape[-1]
    window = 2 * half
    odd_y = lax.rem(lax.axis_index("gy"), 2)
    columns = pl.ds(0, window)
    narrow_outer(
        middle, from_second.at[:2, :half], from_first.at[:2, :half], first.at[:, columns], second.at[:, columns]
    )
    size = notes.shape[0]
    above, below = sides(odd_y, from_first[0, half:, :half], from_second[0, half:, :half])
    for ref in (first, second):
        ref[0, window : window + size] = above
        ref[0, window + size : window + 2 * size] = notes[...]
        ref[0, window + 2 * size :] = below


def narrow_parts(middle, from_second, from_first, first, second_re, second_im, second):
    narrow_outer(middle, from_second, from_first, first, second)
    second_re[0] = second[0]
    second_im[0] = second[1]


def narrow_outer(middle, from_second, from_first, first, second):
    half = first.shape[-1]
    odd_x = lax.rem(lax.axis_index("gx"), 2)
    odd_y = lax.rem(lax.axis_index("gy"), 2)
    for plane in range(middle.shape[0]):
        for received, base in ((from_first, (1 - odd_y) * half), (from_second, odd_y * half)):
            at = pl.ds(pl.multiple_of(base, half), half)
            left = middle[plane, at, :half] + received[plane, :, :half]
            right = middle[plane, at, 3 * half :] + received[plane, :, half:]
            second[plane, at, :], first[plane, at, :] = sides(odd_x, right, left)


def join(middle, received, out, low):
    window = middle.shape[1]
    half = window // 2
    odd_x = lax.rem(lax.axis_index("gx"), 2)
    base = (odd_x if low else 1 - odd_x) * half
    at = pl.ds(pl.multiple_of(half + base, half), half)
    out[...] = middle[:, :, at] + received[:, :window]


def written(value, out, number, sem):
    copy = pltpu.make_async_copy(value, out.at[number], sem)
    copy.start()
    return copy


def update_second(
    object_field, scale, total2_first, total2_second, inner_second, inner_first, out, value, sem
):
    half = scale.shape[-1] // 2
    odd_x = lax.rem(lax.axis_index("gx"), 2)
    odd_y = lax.rem(lax.axis_index("gy"), 2)
    for part in range(2):
        for received, base in ((inner_first, (1 - odd_y) * half), (inner_second, odd_y * half)):
            rows = pl.ds(pl.multiple_of(base, half), half)
            outer = jnp.concatenate(sides(odd_x, total2_first[part, rows], total2_second[part, rows]), axis=1)
            value[part, rows] = object_field[1, part, rows] - (outer + received[2 + part]) * scale[rows]
    written(value, out, 1, sem).wait()


def update_first(
    begun, first1, second1_re, second1_im, object_field, scale, middle1, inner_second, inner_first, out, value, sems
):
    del begun
    window = scale.shape[-1]
    half = window // 2
    odd_x = lax.rem(lax.axis_index("gx"), 2)
    odd_y = lax.rem(lax.axis_index("gy"), 2)
    copies = []
    for part in range(2):
        for received, base in ((inner_first, (1 - odd_y) * half), (inner_second, odd_y * half)):
            rows = pl.ds(pl.multiple_of(base, half), half)
            outer = jnp.concatenate(sides(odd_x, first1[part, rows], (second1_re, second1_im)[part][0, rows]), axis=1)
            total = middle1[part, rows, half : 3 * half] + received[part] + outer
            value[part, rows] = object_field[0, part, rows] - total * scale[rows]
        copies.append(written(value.at[part], out.at[0], part, sems.at[part]))
    for copy in copies:
        copy.wait()


VMEM = pl.BlockSpec(memory_space=pltpu.VMEM)
SMEM = pl.BlockSpec(memory_space=pltpu.SMEM)
ANY = pl.BlockSpec(memory_space=pl.ANY)


def call(body, outs, in_specs, args, scratch=(), out_specs=None, aliases=None, micros=0.0, name=None):
    return pl.pallas_call(
        body,
        out_shape=[x if hasattr(x, "dtype") else jax.ShapeDtypeStruct(x, F32) for x in outs],
        in_specs=in_specs,
        out_specs=out_specs or [VMEM] * len(outs),
        input_output_aliases=aliases or {},
        scratch_shapes=list(scratch),
        compiler_params=pltpu.CompilerParams(vmem_limit_bytes=24 * 1024 * 1024),
        cost_estimate=pl.CostEstimate(flops=int(micros * 1e9), bytes_accessed=1, transcendentals=0),
        name=name,
    )(*args)


def shards(object_field, probe, positions, residual, saved_wave):
    window = probe.shape[-1]
    half = window // 2
    count = positions.shape[0]
    size = notes_size(count)
    table = jnp.asarray(tables(window))
    barrier = lax.optimization_barrier

    def twice(*planes):
        return pltpu.VMEM((*planes, 2 * window + 8, window), F32)

    grads = pltpu.VMEM((2, count, window, window), F32)
    pos_scratch = [pltpu.SMEM(positions.shape, jnp.int32), pltpu.SemaphoreType.DMA]
    fields_shape = (count, 2, window, window)
    wide_shape = (2, window, 2 * window)
    square, strip = (2, half, window), (2, window, half)

    edge_first, edge_second = call(
        edges, [strip] * 2, [VMEM], (object_field,), micros=12.0, name="edges"
    )
    halo_first = swapped(edge_first, "gx", 0)
    halo_second = swapped(edge_second, "gx", 1)

    field, up2, down2, inner2_first, inner2_second, middle2, notes, marks = call(
        detect,
        [fields_shape]
        + [(4, half + size, window)] * 2
        + [square, square, wide_shape, (size, half), jax.ShapeDtypeStruct((2 * count, 8, window), jnp.int32)],
        [ANY] + [VMEM] * 4,
        (positions, residual, saved_wave, table, object_field),
        [twice(count, 2), grads] + pos_scratch,
        micros=12.0, name="detect",
    )
    from_down2 = swapped(down2, "gy", 1)
    from_up2 = swapped(up2, "gy", 0)

    fields, probes = call(
        roll_fields,
        [fields_shape] * 2,
        [ANY] + [VMEM] * 2,
        (positions, field, probe),
        [twice(count + 1, 2)] + pos_scratch,
        micros=0.1, name="roll",
    )
    rows_first, rows_second = call(
        relay,
        [square] * 2,
        [VMEM] * 2,
        (halo_first, halo_second),
        micros=12.0, name="widen",
    )
    from_rows_second = swapped(rows_second, "gy", 1)
    from_rows_first = swapped(rows_first, "gy", 0)

    from_down2, from_up2, fields, probes = barrier((from_down2, from_up2, fields, probes))
    first2, second2 = call(
        narrow_noted,
        [(2, window + 3 * size, half)] * 2,
        [VMEM] * 4,
        (notes, middle2, from_down2, from_up2),
        micros=0.2, name="narrow2",
    )
    from_rows_second, from_rows_first, marks, _ = barrier((from_rows_second, from_rows_first, marks, first2))
    got_first2 = swapped(first2, "gx", 0)
    got_second2 = swapped(second2, "gx", 1)

    outer_first, outer_second, inner_first, inner_second, middle1 = call(
        propagate,
        [square] * 2 + [(4, half, window)] * 2 + [wide_shape],
        [VMEM] * 13,
        (marks, fields, probes, object_field, halo_first, halo_second, from_down2, from_up2)
        + (from_rows_second, from_rows_first, table, inner2_first, inner2_second),
        [pltpu.VMEM(fields_shape, BF16)] * 2 + [grads],
        micros=0.1, name="propagate",
    )
    from_outer_second = swapped(outer_second, "gy", 1)
    from_outer_first = swapped(outer_first, "gy", 0)
    (total2_second,) = call(
        functools.partial(join, low=True), [strip], [VMEM] * 2, (middle2, got_second2), micros=1.0, name="join3"
    )
    (total2_first,) = call(
        functools.partial(join, low=False), [strip], [VMEM] * 2, (middle2, got_first2), micros=0.5, name="join2"
    )
    middle1, total2_first, total2_second = barrier((middle1, total2_first, total2_second))
    first1, second1_re, second1_im = call(
        narrow_parts,
        [strip] + [(1, window, half)] * 2,
        [VMEM] * 3,
        (middle1, from_outer_second, from_outer_first),
        [pltpu.VMEM(strip, F32)],
        micros=0.2, name="narrow1",
    )
    got_first1 = swapped(first1, "gx", 0)
    got_second1_im = around(second1_im, "gx")
    got_second1_re = swapped(second1_re, "gx", 1)
    from_inner_first = swapped(inner_first, "gy", 0)
    from_inner_second = swapped(inner_second, "gy", 1)

    (scale,) = call(
        illuminate,
        [(window, window)],
        [SMEM] + [VMEM] * 5,
        (positions, probe, from_up2, from_down2, got_first2, got_second2),
        [twice(), pltpu.SMEM((8 * size, half), F32), pltpu.SemaphoreType.DMA((4,))],
        micros=2.5, name="illuminate",
    )
    value = pltpu.VMEM(fields_shape[1:], F32)
    (begun,) = call(
        update_second,
        [object_field.shape],
        [VMEM] * 6,
        (object_field, scale, total2_first, total2_second, from_inner_second, from_inner_first),
        [value, pltpu.SemaphoreType.DMA],
        out_specs=[ANY], micros=0.1, name="update2",
    )
    (new_object,) = call(
        update_first,
        [object_field.shape],
        [ANY] + [VMEM] * 8,
        (begun, got_first1, got_second1_re, got_second1_im, object_field, scale, middle1)
        + (from_inner_second, from_inner_first),
        [value, pltpu.SemaphoreType.DMA((2,))],
        out_specs=[ANY], aliases={0: 0}, micros=1.0, name="update",
    )
    return new_object


def solution(mesh):
    placed = (
        P(None, None, "gy", "gx"),
        P(),
        P("gy", "gx", None),
        P("gy", "gx", None, None, None),
        P("gy", "gx", None, None, None),
    )
    return jax.shard_map(
        shards, mesh=mesh, in_specs=placed, out_specs=P(None, None, "gy", "gx"), check_vma=False
    )
```
